128 devices in a mesh: ctx: 8 (over y, core), seq: 16 (over x, z).
Axes of the slice: x: 4, y: 4, z: 4, core: 2. Of those that a mesh axis runs over, the one named last changes fastest.
Arguments:
- tokens: bfloat16 [131072, 1024], P(('ctx', 'seq')), parts along dimension 0, may hold values from -16 to 16
- ln_gain: float32 [1024], replicated, may hold values from 0.5 to 1.5
- post_gain: float32 [1024], replicated, may hold values from 0.25 to 1.75
- w_query: bfloat16 [1024, 1024], replicated, may hold values from -32 to 32
- w_key: bfloat16 [1024, 1024], replicated, may hold values from -1 to 1
- w_value: bfloat16 [1024, 1024], replicated, may hold values from -0.1875 to 0.1875
- w_out: bfloat16 [1024, 1024], replicated, may hold values from -0.1875 to 0.1875
Outputs:
- latent_out: bfloat16 [8192, 1024], P(('ctx', 'seq')), parts along dimension 0
The draws below stay inside these ranges and needn't reach their ends.
There are 8 independent parts, one for each index of `ctx`. The reference program is written for one: setup_inputs(seed, part) draws one part's arguments, and reference() takes and returns one part's arrays. A program takes and returns all parts, laid end to end along the dimension named above; an argument that names none is the same for every part. Nothing has to cross between parts.
All inputs are finite; a program needn't handle non-finite values.
Results may differ from the reference program's by a relative error of at most 0.018.
Values may be sent and summed in bfloat16 or wider, within the bound.
No kernel may reach another device: no remote copies, remote signals or barrier semaphores. Data moves between devices by JAX's collectives and lax.ppermute only.
A program may use at most 320 MiB of HBM per device.

```python
import jax
import jax.numpy as jnp
from jax import lax

D = 1024
HEADS = 16
HEAD_DIM = 64
LATENTS = 1024
TOK_DEV = 1024
TOKENS = 16384


def key_matrix(key):
    return jax.random.normal(key, (D, D), jnp.float32) * D ** (-0.5)


def draw_w_key(key, part):
    return key_matrix(key).astype(jnp.bfloat16)


def draw_w_query(key, part):
    key = jax.random.fold_in(key, 7)
    noise = jax.random.normal(key, (D, D), jnp.float32) * D ** (-0.5)
    result = noise
    return result.astype(jnp.bfloat16)


def draw_tokens(key, part):
    key = jax.random.fold_in(key, 3)
    result = jax.random.normal(key, (TOKENS, D), jnp.float32)
    return result.astype(jnp.bfloat16)


def centred(stream_key, extent, spread, reach, held_as=jnp.bfloat16):
    entries = jax.random.normal(stream_key, extent, jnp.float32) * spread
    return jnp.minimum(jnp.maximum(entries, -reach), reach).astype(held_as)


def setup_inputs(seed: int = 0, part: int = 0) -> dict:
    seeds = jax.random.split(jax.random.key(seed), 8)
    own_keys = jax.random.split(jax.random.fold_in(seeds[7], part), 8)
    return {
        "tokens": draw_tokens(jax.random.fold_in(jax.random.fold_in(seeds[7], part), 71), part),
        "ln_gain": jnp.clip(1.0 + 0.1 * jax.random.normal(seeds[1], (D,), jnp.float32), 0.5, 1.5),
        "post_gain": jnp.clip(1.0 + 0.15 * jax.random.normal(seeds[2], (D,), jnp.float32), 0.25, 1.75),
        "w_query": draw_w_query(jax.random.fold_in(seeds[7], 71), part),
        "w_key": draw_w_key(jax.random.fold_in(seeds[7], 71), part),
        "w_value": centred(seeds[5], (D, D), D ** -0.5, 0.1875),
        "w_out": centred(seeds[6], (D, D), D ** -0.5, 0.1875),
    }


def rms_rows(rows, gain):
    wide = rows.astype(jnp.float32)
    scale = lax.rsqrt(lax.optimization_barrier(jnp.mean(wide * wide, axis=-1, keepdims=True)) + 1e-06)
    return (wide * scale * gain).astype(jnp.bfloat16)

def reference(tokens, ln_gain, post_gain, w_query, w_key, w_value, w_out):
    normed = rms_rows(tokens, ln_gain)
    keys = jnp.dot(normed, w_key, preferred_element_type=jnp.float32).astype(jnp.bfloat16)
    values = jnp.dot(normed, w_value, preferred_element_type=jnp.float32).astype(jnp.bfloat16)
    latent_rows = tokens[TOKENS - LATENTS:]
    queries = jnp.dot(normed[TOKENS - LATENTS:], w_query, preferred_element_type=jnp.float32).astype(jnp.bfloat16)
    blocks = TOKENS // TOK_DEV
    key_pos = jnp.arange(TOKENS, dtype=jnp.int32).reshape(blocks, TOK_DEV)
    query_pos = TOKENS - LATENTS + jnp.arange(LATENTS, dtype=jnp.int32)
    allowed = key_pos[None, :, :] <= query_pos[:, None, None]
    factor = HEAD_DIM ** (-0.5)

    def one_head(head):
        start = (head * HEAD_DIM).astype(jnp.int32)
        query_h = lax.dynamic_slice_in_dim(queries, start, HEAD_DIM, 1)
        key_h = lax.dynamic_slice_in_dim(keys, start, HEAD_DIM, 1)
        value_h = lax.dynamic_slice_in_dim(values, start, HEAD_DIM, 1)
        scores = lax.dot_general(query_h, key_h, (((1,), (1,)), ((), ())), preferred_element_type=jnp.float32) * factor
        scores = jnp.where(allowed, scores.reshape(LATENTS, blocks, TOK_DEV), jnp.float32(-1e+30))
        block_max = lax.optimization_barrier(jnp.max(scores, axis=-1))
        probs = jnp.exp(scores - block_max[..., None])
        weights = probs.astype(jnp.bfloat16)
        block_sum = lax.optimization_barrier(jnp.sum(probs, axis=-1))
        value_blocks = value_h.reshape(blocks, TOK_DEV, HEAD_DIM).astype(jnp.float32)
        block_mix = jnp.einsum('lnt,nte->lne', weights.astype(jnp.float32), value_blocks)
        row_max = lax.optimization_barrier(jnp.max(block_max, axis=-1))
        rescale = jnp.exp(block_max - row_max[:, None])
        totals = lax.optimization_barrier(jnp.sum(block_sum * rescale, axis=-1))
        mixture = lax.optimization_barrier(jnp.sum(block_mix * rescale[..., None], axis=1))
        return (mixture / totals[:, None]).astype(jnp.bfloat16)
    per_head = lax.map(one_head, jnp.arange(HEADS, dtype=jnp.int32))
    attended = jnp.transpose(per_head, (1, 0, 2)).reshape(LATENTS, D)
    post = rms_rows(attended, post_gain)
    mixed = latent_rows.astype(jnp.float32) + jnp.dot(post, w_out, preferred_element_type=jnp.float32)
    return mixed.astype(jnp.bfloat16)
```

```python
import functools

import jax
import jax.numpy as jnp
from jax import lax
from jax.experimental import pallas as pl
from jax.experimental.pallas import tpu as pltpu
from jax.sharding import PartitionSpec as P

D = 1024
HEADS = 16
HEAD_DIM = 64
LATENTS = 1024
CHUNKS = 2
LOG2E = 1.4426950408889634
EXP2_SCALE = LOG2E * HEAD_DIM ** (-0.5)
MASKED = -1e30
WIDE = D + 128


def rms_rows(rows, gain):
    wide = rows.astype(jnp.float32)
    scale = lax.rsqrt(jnp.mean(wide * wide, axis=-1, keepdims=True) + 1e-06)
    return (wide * scale * gain).astype(jnp.bfloat16)


def kv_kernel(tokens, gain, w_key, w_value, keys, values, normed):
    @pl.when(pl.program_id(0) == 0)
    def _():
        normed[...] = rms_rows(tokens[...], gain[...])

    rows = normed[...]
    keys[...] = jnp.dot(rows, w_key[...], preferred_element_type=jnp.float32).astype(jnp.bfloat16)
    values[...] = jnp.dot(rows, w_value[...], preferred_element_type=jnp.float32).astype(jnp.bfloat16)


def project_kv(tokens, gain, w_key, w_value):
    rows = tokens.shape[0]
    cols = 256
    whole = lambda c: (0, 0)
    block = lambda c: (0, c)
    return pl.pallas_call(
        kv_kernel,
        grid=(D // cols,),
        out_shape=(jax.ShapeDtypeStruct((rows, D), jnp.bfloat16),) * 2,
        in_specs=[
            pl.BlockSpec((rows, D), whole),
            pl.BlockSpec((1, D), whole),
            pl.BlockSpec((D, cols), block),
            pl.BlockSpec((D, cols), block),
        ],
        out_specs=(pl.BlockSpec((rows, cols), block),) * 2,
        scratch_shapes=[pltpu.VMEM((rows, D), jnp.bfloat16)],
        compiler_params=pltpu.CompilerParams(vmem_limit_bytes=56 * 2**20),
        cost_estimate=pl.CostEstimate(flops=4 * rows * D * D, bytes_accessed=10 * rows * D, transcendentals=0),
        name="project_kv",
    )(tokens, gain, w_key, w_value)


def attend_kernel(chunk, owned, flag, queries, keys, values, out):
    rows = queries.shape[0]
    count = keys.shape[0]
    step = pl.program_id(0)
    pairs = HEADS // 2
    part = owned // CHUNKS
    low = lax.broadcasted_iota(jnp.int32, (1, 128), 1) < HEAD_DIM

    def attention(causal):
        lane = lax.broadcasted_iota(jnp.int32, (rows, 128), 1)
        lse = jnp.zeros((rows, 128), jnp.float32)
        ones = jnp.ones((count, 128), jnp.bfloat16)
        if causal:
            key_pos = lax.broadcasted_iota(jnp.int32, (rows, count), 1)
            row = step * rows + lax.broadcasted_iota(jnp.int32, (rows, count), 0)
            query_pos = (row // part) * owned + chunk * part + row % part
            allowed = key_pos <= query_pos
            allowed = jnp.concatenate([allowed, allowed], axis=0)

        def scores_of(pair):
            at = slice(pair * 128, (pair + 1) * 128)
            query = queries[:, at]
            none = jnp.zeros_like(query)
            both = jnp.concatenate([jnp.where(low, query, none), jnp.where(low, none, query)], axis=0)
            scores = lax.dot_general(
                both, keys[:, at], (((1,), (1,)), ((), ())), preferred_element_type=jnp.float32
            )
            return jnp.where(allowed, scores, MASKED) if causal else scores

        ahead = scores_of(0)
        for pair in range(pairs):
            at = slice(pair * 128, (pair + 1) * 128)
            scores = ahead
            if pair + 1 < pairs:
                ahead = scores_of(pair + 1)
            top = jnp.max(scores, axis=-1, keepdims=True)
            weights = jnp.exp2((scores - top) * EXP2_SCALE).astype(jnp.bfloat16)
            mixed = jnp.dot(
                weights,
                jnp.concatenate([values[:, at], ones], axis=1),
                preferred_element_type=jnp.float32,
            )
            mix, total = mixed[:, 0:128], mixed[:, 128:256]
            both = jnp.where(low, mix[:rows], mix[rows:]) / jnp.where(low, total[:rows], total[rows:])
            out[:, at] = both.astype(jnp.bfloat16)
            level = top * EXP2_SCALE + jnp.log2(total)
            lse = jnp.where(lane == 2 * pair, level[:rows], lse)
            lse = jnp.where(lane == 2 * pair + 1, level[rows:], lse)
        first = lse.astype(jnp.bfloat16).astype(jnp.float32)
        second = (lse - first).astype(jnp.bfloat16).astype(jnp.float32)
        third = lse - first - second
        pieces = first + pltpu.roll(second, HEADS, 1) + pltpu.roll(third, 2 * HEADS, 1)
        out[:, D:WIDE] = pieces.astype(jnp.bfloat16)

    @pl.when(flag[0] == 0)
    def _():
        attention(False)

    @pl.when(flag[0] != 0)
    def _():
        attention(True)


def attend(chunk, owned, is_last, queries, keys, values):
    count = queries.shape[0]
    rows = 256
    whole = lambda c: (0, 0)
    block = lambda c: (c, 0)
    return pl.pallas_call(
        functools.partial(attend_kernel, chunk, owned),
        grid=(count // rows,),
        out_shape=jax.ShapeDtypeStruct((count, WIDE), jnp.bfloat16),
        in_specs=[
            pl.BlockSpec(memory_space=pltpu.SMEM),
            pl.BlockSpec((rows, D), block),
            pl.BlockSpec(keys.shape, whole),
            pl.BlockSpec(values.shape, whole),
        ],
        out_specs=pl.BlockSpec((rows, WIDE), block),
        compiler_params=pltpu.CompilerParams(vmem_limit_bytes=56 * 2**20),
        cost_estimate=pl.CostEstimate(
            flops=16 * count * D * D, bytes_accessed=8 * D * D, transcendentals=HEADS * count * D
        ),
        name="attend_%d" % chunk,
    )(is_last, queries, keys, values)


def finish_kernel(*refs):
    parts = refs[:CHUNKS]
    residual, gain, w_out, out = refs[CHUNKS:]
    count, part, _ = parts[0].shape
    head = lax.broadcasted_iota(jnp.int32, (128, D), 0)
    column = lax.broadcasted_iota(jnp.int32, (128, D), 1)
    spread = (column // HEAD_DIM == head).astype(jnp.bfloat16)
    spread = jnp.concatenate([spread, spread], axis=0)
    lane = lax.broadcasted_iota(jnp.int32, (count * part, 128), 1)
    for chunk in range(CHUNKS):
        pieces = parts[chunk][:, :, D:WIDE].astype(jnp.float32).reshape(count * part, 128)
        level = pieces + pltpu.roll(pieces, 128 - HEADS, 1) + pltpu.roll(pieces, 128 - 2 * HEADS, 1)
        level = jnp.where(lane < HEADS, level, 0.0).reshape(count, part, 128)
        weight = jnp.exp2(level - jnp.max(level, axis=0, keepdims=True))
        weight = weight / jnp.sum(weight, axis=0, keepdims=True)
        weight = weight.reshape(count * part, 128)
        weight_high = weight.astype(jnp.bfloat16)
        weight_low = (weight - weight_high.astype(jnp.float32)).astype(jnp.bfloat16)
        wide = jnp.dot(
            jnp.concatenate([weight_high, weight_low], axis=1), spread, preferred_element_type=jnp.float32
        ).reshape(count, part, D)
        mix = jnp.sum(wide * parts[chunk][:, :, 0:D].astype(jnp.float32), axis=0)
        attended = mix.astype(jnp.bfloat16)
        post = rms_rows(attended, gain[...])
        at = slice(chunk * part, (chunk + 1) * part)
        mixed = residual[at, :].astype(jnp.float32) + jnp.dot(
            post, w_out[...], preferred_element_type=jnp.float32
        )
        out[at, :] = mixed.astype(jnp.bfloat16)


def finish(parts, residual, gain, w_out):
    return pl.pallas_call(
        finish_kernel,
        out_shape=jax.ShapeDtypeStruct(residual.shape, jnp.bfloat16),
        compiler_params=pltpu.CompilerParams(vmem_limit_bytes=48 * 2**20),
        name="finish",
    )(*parts, residual, gain, w_out)


def local(tokens, ln_gain, post_gain, w_query, w_key, w_value, w_out):
    count = lax.axis_size("seq")
    me = lax.axis_index("seq")
    owned = LATENTS // count
    part = owned // CHUNKS
    last = me == count - 1
    gain = ln_gain.reshape(1, D)
    sent = [
        lax.ppermute(tokens[to * owned : (to + 1) * owned], "seq", [(count - 1, to)])
        for to in range(count - 1)
    ]
    own_rows = jnp.where(last, tokens[(count - 1) * owned :], sum(sent))
    queries = jnp.dot(
        rms_rows(own_rows, ln_gain), w_query, preferred_element_type=jnp.float32
    ).astype(jnp.bfloat16)
    keys, values = project_kv(tokens, gain, w_key, w_value)
    flag = last.astype(jnp.int32).reshape(1)
    parts = []
    for chunk in range(CHUNKS):
        mine = queries[chunk * part : (chunk + 1) * part]
        tiled = jnp.broadcast_to(mine[None], (count, part, D))
        rows = lax.all_to_all(tiled, "seq", 0, 0).reshape(count * part, D)
        mixed = attend(chunk, owned, flag, rows, keys, values)
        parts.append(lax.all_to_all(mixed.reshape(count, part, WIDE), "seq", 0, 0))
    return finish(parts, own_rows, post_gain.reshape(1, D), w_out)


def solution(mesh):
    return jax.shard_map(
        local,
        mesh=mesh,
        in_specs=(P(("ctx", "seq"), None), P(), P(), P(), P(), P(), P()),
        out_specs=P(("ctx", "seq"), None),
        check_vma=False,
    )
```

```python
import functools

import jax
import jax.numpy as jnp
from jax import lax
from jax.experimental import pallas as pl
from jax.experimental.pallas import tpu as pltpu
from jax.sharding import PartitionSpec as P

D = 1024
HEADS = 16
HEAD_DIM = 64
PAIRS = HEADS // 2
LATENTS = 1024
PART = 16
LOG2E = 1.4426950408889634
EXP2_SCALE = LOG2E * HEAD_DIM ** (-0.5)
MASKED = -1e30
WIDE = D + 128
MIB = 2**20

BUNDLES = ((3, 0, 2, 1), (11, 8, 10, 9), (12, 13, 4, 5), (14, 6, 7))


def rms_rows(rows, gain):
    wide = rows.astype(jnp.float32)
    scale = lax.rsqrt(jnp.mean(wide * wide, axis=-1, keepdims=True) + 1e-06)
    return (wide * scale * gain).astype(jnp.bfloat16)


def kv_kernel(tokens, gain, w_key, w_value, keys, values, normed):
    @pl.when(pl.program_id(0) == 0)
    def _():
        normed[...] = rms_rows(tokens[...], gain[...])

    rows = normed[...]
    keys[...] = jnp.dot(rows, w_key[...], preferred_element_type=jnp.float32).astype(jnp.bfloat16)
    values[...] = jnp.dot(rows, w_value[...], preferred_element_type=jnp.float32).astype(jnp.bfloat16)


def project_kv(tokens, gain, w_key, w_value):
    rows = tokens.shape[0]
    cols = 256
    whole = lambda c: (0, 0)
    block = lambda c: (0, c)
    return pl.pallas_call(
        kv_kernel,
        grid=(D // cols,),
        out_shape=(jax.ShapeDtypeStruct((rows, D), jnp.bfloat16),) * 2,
        in_specs=[
            pl.BlockSpec((rows, D), whole, pipeline_mode=pl.Buffered(1)),
            pl.BlockSpec((1, D), whole),
            pl.BlockSpec((D, cols), block),
            pl.BlockSpec((D, cols), block),
        ],
        out_specs=(pl.BlockSpec((rows, cols), block),) * 2,
        scratch_shapes=[pltpu.VMEM((rows, D), jnp.bfloat16)],
        compiler_params=pltpu.CompilerParams(vmem_limit_bytes=20 * MIB),
        cost_estimate=pl.CostEstimate(flops=4 * rows * D * D, bytes_accessed=10 * rows * D, transcendentals=0),
        name="project_kv",
    )(tokens, gain, w_key, w_value)


def query_kernel(count, gain, w_query, *refs):
    parts, (own, *tiled) = refs[:5], refs[5:]
    rows = parts[0][...].astype(jnp.float32)
    for part in parts[1:]:
        rows = rows + part[...].astype(jnp.float32)
    rows = rows.astype(jnp.bfloat16)
    own[...] = rows
    queries = jnp.dot(
        rms_rows(rows, gain[...]), w_query[...], preferred_element_type=jnp.float32
    ).astype(jnp.bfloat16)
    begin = 0
    for each in tiled:
        end = begin + each.shape[1]
        for to in range(count):
            each[to] = queries[begin:end]
        begin = end


def project_queries(count, gain, w_query, parts):
    rows = parts[0].shape[0]
    return pl.pallas_call(
        functools.partial(query_kernel, count),
        out_shape=(jax.ShapeDtypeStruct((rows, D), jnp.bfloat16),)
        + tuple(jax.ShapeDtypeStruct((count, each, D), jnp.bfloat16) for each in (PART, rows - PART)),
        compiler_params=pltpu.CompilerParams(vmem_limit_bytes=16 * MIB),
        cost_estimate=pl.CostEstimate(flops=2 * rows * D * D, bytes_accessed=4 * D * D, transcendentals=0),
        name="project_queries",
    )(gain, w_query, *parts)


def attend_kernel(first, owned, flag, queries, keys, values, out, s_a, s_b, p_a, p_b, top_a, top_b, lse):
    group, part, _ = queries.shape
    rows = group * part
    count = keys.shape[0]
    offset = (first + pl.program_id(0)) * part
    low = lax.broadcasted_iota(jnp.int32, (1, 128), 1) < HEAD_DIM
    sub = 32

    def score(pair, s):
        at = pl.ds(pl.multiple_of(pair * 128, 128), 128)
        query = queries[:, :, at].reshape(rows, 128)
        none = jnp.zeros_like(query)
        both = jnp.concatenate([jnp.where(low, query, none), jnp.where(low, none, query)], axis=0)
        s[...] = lax.dot_general(
            both, keys[:, at], (((1,), (1,)), ((), ())), preferred_element_type=jnp.float32
        )

    def soften(causal, s, p, top):
        for begin in range(0, 2 * rows, sub):
            at = slice(begin, begin + sub)
            begin = begin % rows
            span = count
            if causal:
                last = (begin + sub - 1) // part * owned + owned
                span = min(count, -(-last // 128) * 128)
            block = s[at, 0:span]
            if causal:
                row = begin + lax.broadcasted_iota(jnp.int32, (sub, span), 0)
                query_pos = row // part * owned + offset + row % part
                key_pos = lax.broadcasted_iota(jnp.int32, (sub, span), 1)
                block = jnp.where(key_pos <= query_pos, block, MASKED)
            most = jnp.max(block, axis=-1, keepdims=True)
            p[at, 0:span] = jnp.exp2((block - most) * EXP2_SCALE).astype(jnp.bfloat16)
            if span < count:
                p[at, span:count] = jnp.zeros((sub, count - span), jnp.bfloat16)
            top[at, :] = jnp.broadcast_to(most, (sub, 128))

    def blend(pair, p, top):
        at = pl.ds(pl.multiple_of(jnp.maximum(pair, 0) * 128, 128), 128)
        ones = jnp.ones((count, 128), jnp.bfloat16)
        mixed = jnp.dot(
            p[...], jnp.concatenate([values[:, at], ones], axis=1), preferred_element_type=jnp.float32
        )
        mix, total = mixed[:, 0:128], mixed[:, 128:256]
        both = jnp.where(low, mix[:rows], mix[rows:]) / jnp.where(low, total[:rows], total[rows:])
        out[:, :, at] = both.astype(jnp.bfloat16).reshape(group, part, 128)
        level = top[...] * EXP2_SCALE + jnp.log2(total)
        lane = lax.broadcasted_iota(jnp.int32, (rows, 128), 1)
        held = jnp.where(lane == 2 * pair, level[:rows], lse[...])
        lse[...] = jnp.where(lane == 2 * pair + 1, level[rows:], held)

    def attention(causal):
        score(0, s_a)
        score(1, s_b)
        soften(causal, s_a, p_a, top_a)

        def two_pairs(i, _):
            score(2 * i, s_a)
            blend(2 * i - 2, p_a, top_a)
            soften(causal, s_b, p_b, top_b)
            score(2 * i + 1, s_b)
            blend(2 * i - 1, p_b, top_b)
            soften(causal, s_a, p_a, top_a)
            return 0

        lse[...] = jnp.zeros_like(lse)
        lax.fori_loop(1, PAIRS // 2, two_pairs, 0)
        blend(PAIRS - 2, p_a, top_a)
        soften(causal, s_b, p_b, top_b)
        blend(PAIRS - 1, p_b, top_b)
        level = lse[...]
        one = level.astype(jnp.bfloat16).astype(jnp.float32)
        two = (level - one).astype(jnp.bfloat16).astype(jnp.float32)
        three = level - one - two
        pieces = one + pltpu.roll(two, HEADS, 1) + pltpu.roll(three, 2 * HEADS, 1)
        out[:, :, D:WIDE] = pieces.astype(jnp.bfloat16).reshape(group, part, 128)

    @pl.when(flag[0] == 0)
    def _():
        attention(False)

    @pl.when(flag[0] != 0)
    def _():
        attention(True)


def attend(first, begin, steps, owned, is_last, queries, keys, values):
    group = queries.shape[0]
    rows = group * PART
    count = keys.shape[0]
    whole = lambda c: (0, 0)
    return pl.pallas_call(
        functools.partial(attend_kernel, first, owned),
        grid=(steps,),
        out_shape=jax.ShapeDtypeStruct((group, steps * PART, WIDE), jnp.bfloat16),
        in_specs=[
            pl.BlockSpec(memory_space=pltpu.SMEM),
            pl.BlockSpec((group, PART, D), lambda c: (0, begin + c, 0)),
            pl.BlockSpec((count, D), whole, pipeline_mode=pl.Buffered(1)),
            pl.BlockSpec((count, D), whole, pipeline_mode=pl.Buffered(1)),
        ],
        out_specs=pl.BlockSpec((group, PART, WIDE), lambda c: (0, c, 0)),
        scratch_shapes=[
            pltpu.VMEM((2 * rows, count), jnp.float32),
            pltpu.VMEM((2 * rows, count), jnp.float32),
            pltpu.VMEM((2 * rows, count), jnp.bfloat16),
            pltpu.VMEM((2 * rows, count), jnp.bfloat16),
            pltpu.VMEM((2 * rows, 128), jnp.float32),
            pltpu.VMEM((2 * rows, 128), jnp.float32),
            pltpu.VMEM((rows, 128), jnp.float32),
        ],
        compiler_params=pltpu.CompilerParams(vmem_limit_bytes=28 * MIB),
        cost_estimate=pl.CostEstimate(
            flops=16 * steps * rows * D * D,
            bytes_accessed=8 * D * D,
            transcendentals=HEADS * steps * rows * D,
        ),
        name="attend_%d" % first,
    )(is_last, queries, keys, values)


def finish_kernel(number, *refs):
    parts, (own, gain, w_out, out) = refs[:number], refs[number:]
    head = lax.broadcasted_iota(jnp.int32, (128, D), 0)
    column = lax.broadcasted_iota(jnp.int32, (128, D), 1)
    spread = (column // HEAD_DIM == head).astype(jnp.bfloat16)
    spread = jnp.concatenate([spread, spread], axis=0)
    posts = []
    for each in parts:
        count, part, _ = each.shape
        lane = lax.broadcasted_iota(jnp.int32, (count * part, 128), 1)
        pieces = each[:, :, D:WIDE].astype(jnp.float32).reshape(count * part, 128)
        level = pieces + pltpu.roll(pieces, 128 - HEADS, 1) + pltpu.roll(pieces, 128 - 2 * HEADS, 1)
        level = jnp.where(lane < HEADS, level, 0.0).reshape(count, part, 128)
        weight = jnp.exp2(level - jnp.max(level, axis=0, keepdims=True))
        weight = weight / jnp.sum(weight, axis=0, keepdims=True)
        weight = weight.reshape(count * part, 128)
        high = weight.astype(jnp.bfloat16)
        rest = (weight - high.astype(jnp.float32)).astype(jnp.bfloat16)
        wide = jnp.dot(
            jnp.concatenate([high, rest], axis=1), spread, preferred_element_type=jnp.float32
        ).reshape(count, part, D)
        mix = jnp.sum(wide * each[:, :, 0:D].astype(jnp.float32), axis=0)
        posts.append(rms_rows(mix.astype(jnp.bfloat16), gain[...]))
    mixed = own[...].astype(jnp.float32) + jnp.dot(
        jnp.concatenate(posts, axis=0), w_out[...], preferred_element_type=jnp.float32
    )
    out[...] = mixed.astype(jnp.bfloat16)


def finish(parts, own, gain, w_out):
    rows = own.shape[0]
    return pl.pallas_call(
        functools.partial(finish_kernel, len(parts)),
        out_shape=jax.ShapeDtypeStruct((rows, D), jnp.bfloat16),
        compiler_params=pltpu.CompilerParams(vmem_limit_bytes=28 * MIB),
        cost_estimate=pl.CostEstimate(flops=4 * rows * D * D, bytes_accessed=8 * D * D, transcendentals=0),
        name="finish",
    )(*parts, own, gain, w_out)


def pack_kernel(owned, source, flag, tokens, own, *bundles):
    def block(to):
        return tokens[to * owned : (to + 1) * owned, :]

    mine = block(source)
    own[...] = jnp.where(flag[0] != 0, mine, jnp.zeros_like(mine))
    for members, bundle in zip(BUNDLES, bundles):
        for place in range(4):
            at = slice(place * owned, (place + 1) * owned)
            bundle[at, :] = block(members[min(place, len(members) - 1)])


def relay_kernel(*refs):
    bundles, outs = refs[:4], refs[4:]
    rows = outs[0].shape[0]
    for place, out in enumerate(outs):
        at = slice(place * rows, (place + 1) * rows)
        total = bundles[0][at, :].astype(jnp.float32)
        for bundle in bundles[1:]:
            total = total + bundle[at, :].astype(jnp.float32)
        out[...] = total.astype(jnp.bfloat16)


def scatter(tokens, owned, source, flag, beside):
    limit = pltpu.CompilerParams(vmem_limit_bytes=16 * MIB)
    block = jax.ShapeDtypeStruct((owned, D), jnp.bfloat16)
    smem = pl.BlockSpec(memory_space=pltpu.SMEM)
    vmem = pl.BlockSpec(memory_space=pltpu.VMEM)
    own, *bundles = pl.pallas_call(
        functools.partial(pack_kernel, owned, source),
        out_shape=(block,) + (jax.ShapeDtypeStruct((4 * owned, D), jnp.bfloat16),) * 4,
        in_specs=[smem, vmem],
        compiler_params=limit,
        cost_estimate=pl.CostEstimate(flops=0, bytes_accessed=8 * D * D, transcendentals=0),
        name="pack",
    )(flag, tokens)
    bundles = [
        lax.ppermute(bundle, "seq", [(source, members[0])]) for members, bundle in zip(BUNDLES, bundles)
    ]
    bundles, _ = lax.optimization_barrier((bundles, beside))
    kept, *passed = pl.pallas_call(
        relay_kernel,
        out_shape=(block,) * 4,
        compiler_params=limit,
        cost_estimate=pl.CostEstimate(flops=0, bytes_accessed=4 * D * D, transcendentals=0),
        name="relay",
    )(*bundles)
    parts = [own, kept]
    for place in range(1, 4):
        pairs = [(members[0], members[place]) for members in BUNDLES if place < len(members)]
        parts.append(lax.ppermute(passed[place - 1], "seq", pairs))
    return parts


def local(tokens, ln_gain, post_gain, w_query, w_key, w_value, w_out):
    count = lax.axis_size("seq")
    last = lax.axis_index("seq") == count - 1
    flag = last.astype(jnp.int32).reshape(1)
    owned = LATENTS // count
    gain = ln_gain.reshape(1, D)
    keys, values = project_kv(tokens, gain, w_key, w_value)
    parts = scatter(tokens, owned, count - 1, flag, keys)
    own, tiled_a, tiled_b = project_queries(count, gain, w_query, parts)
    rows_a = lax.all_to_all(tiled_a, "seq", 0, 0)
    rows_a, tiled_b = lax.optimization_barrier((rows_a, tiled_b))
    rows_b = lax.all_to_all(tiled_b, "seq", 0, 0)
    mixed_a = attend(0, 0, 1, owned, flag, rows_a, keys, values)
    rows_b, _ = lax.optimization_barrier((rows_b, mixed_a))
    mixed_b = attend(1, 0, 2, owned, flag, rows_b, keys, values)
    rows_c, _ = lax.optimization_barrier((rows_b, mixed_b))
    mixed_c = attend(3, 2, 1, owned, flag, rows_c, keys, values)
    mixed = [lax.all_to_all(each, "seq", 0, 0) for each in (mixed_a, mixed_b, mixed_c)]
    return finish(mixed, own, post_gain.reshape(1, D), w_out)


def solution(mesh):
    return jax.shard_map(
        local,
        mesh=mesh,
        in_specs=(P(("ctx", "seq"), None), P(), P(), P(), P(), P(), P()),
        out_specs=P(("ctx", "seq"), None),
        check_vma=False,
    )
```

```python
import functools

import jax
import jax.numpy as jnp
from jax import lax
from jax.experimental import pallas as pl
from jax.experimental.pallas import tpu as pltpu
from jax.sharding import PartitionSpec as P

D = 1024
HEADS = 16
HEAD_DIM = 64
PAIRS = HEADS // 2
LATENTS = 1024
PART = 16
LOG2E = 1.4426950408889634
EXP2_SCALE = LOG2E * HEAD_DIM ** (-0.5)
MASKED = -1e30
WIDE = D + 128
MIB = 2**20

BUNDLES = ((3, 0, 2, 1), (11, 8, 10, 9), (12, 13, 4, 5), (14, 6, 7))


def rms_rows(rows, gain):
    wide = rows.astype(jnp.float32)
    scale = lax.rsqrt(jnp.mean(wide * wide, axis=-1, keepdims=True) + 1e-06)
    return (wide * scale * gain).astype(jnp.bfloat16)


def project_kernel(tokens, gain, weight, out, normed):
    @pl.when(pl.program_id(0) == 0)
    def _():
        normed[...] = rms_rows(tokens[...], gain[...])

    out[...] = jnp.dot(normed[...], weight[...], preferred_element_type=jnp.float32).astype(jnp.bfloat16)


def project(tokens, gain, weight, name):
    rows = tokens.shape[0]
    cols = 256
    whole = lambda c: (0, 0)
    block = lambda c: (0, c)
    return pl.pallas_call(
        project_kernel,
        grid=(D // cols,),
        out_shape=jax.ShapeDtypeStruct((rows, D), jnp.bfloat16),
        in_specs=[
            pl.BlockSpec((rows, D), whole, pipeline_mode=pl.Buffered(1)),
            pl.BlockSpec((1, D), whole),
            pl.BlockSpec((D, cols), block),
        ],
        out_specs=pl.BlockSpec((rows, cols), block),
        scratch_shapes=[pltpu.VMEM((rows, D), jnp.bfloat16)],
        compiler_params=pltpu.CompilerParams(vmem_limit_bytes=56 * MIB),
        cost_estimate=pl.CostEstimate(flops=2 * rows * D * D, bytes_accessed=6 * rows * D, transcendentals=0),
        name=name,
    )(tokens, gain, weight)


def query_kernel(count, number, gain, w_query, *refs):
    parts, (own, *tiled) = refs[:number], refs[number:]
    rows = parts[0][...].reshape(own.shape).astype(jnp.float32)
    for part in parts[1:]:
        rows = rows + part[...].astype(jnp.float32)
    rows = rows.astype(jnp.bfloat16)
    own[...] = rows
    queries = jnp.dot(
        rms_rows(rows, gain[...]), w_query[...], preferred_element_type=jnp.float32
    ).astype(jnp.bfloat16)
    begin = 0
    for each in tiled:
        end = begin + each.shape[1]
        for to in range(count):
            each[to] = queries[begin:end]
        begin = end


def project_queries(count, gain, w_query, parts, sizes):
    rows = sum(sizes)
    vmem = pl.BlockSpec(memory_space=pltpu.VMEM)
    specs = [vmem] * len(parts)
    if parts[0].ndim == 3:
        specs = [pl.BlockSpec((1, rows, D), lambda c: (count - 1, 0, 0))]
    return pl.pallas_call(
        functools.partial(query_kernel, count, len(parts)),
        grid=(1,),
        out_shape=(jax.ShapeDtypeStruct((rows, D), jnp.bfloat16),)
        + tuple(jax.ShapeDtypeStruct((count, each, D), jnp.bfloat16) for each in sizes),
        in_specs=[vmem, vmem] + specs,
        out_specs=(vmem,) * (1 + len(sizes)),
        compiler_params=pltpu.CompilerParams(vmem_limit_bytes=24 * MIB),
        cost_estimate=pl.CostEstimate(flops=2 * rows * D * D, bytes_accessed=4 * D * D, transcendentals=0),
        name="project_queries_%d" % rows,
    )(gain, w_query, *parts)


def attend_kernel(first, owned, aliased, flag, queries, keys, values, *refs):
    out, s, p, top, halves, lse = refs[aliased], refs[aliased + 1 : aliased + 4], *refs[aliased + 4 :]
    group, part, _ = queries.shape
    rows = group * part
    count = keys.shape[0]
    offset = (first + pl.program_id(0)) * part
    low = lax.broadcasted_iota(jnp.int32, (1, 128), 1) < HEAD_DIM
    sub = 32
    quarters = 4

    def at_pair(pair):
        return slice(pair * 128, (pair + 1) * 128)

    def score(pair, quarter):
        span = count // quarters
        query = queries[:, :, at_pair(pair)].reshape(rows, 128)
        none = jnp.zeros_like(query)
        both = jnp.concatenate([jnp.where(low, query, none), jnp.where(low, none, query)], axis=0)
        at = slice(quarter * span, (quarter + 1) * span)
        s[pair % 3][:, at] = lax.dot_general(
            both, keys[at, at_pair(pair)], (((1,), (1,)), ((), ())), preferred_element_type=jnp.float32
        )

    def blocks(causal, pair, quarter):
        span = 2 * rows // quarters
        for begin in range(quarter * span, (quarter + 1) * span, sub):
            free = some = count
            if causal:
                owner = begin % rows // part
                free = owner * owned // 128 * 128
                some = min(count, -(-(owner + sub // part) * owned // 128) * 128)
            yield slice(begin, begin + sub), free, some

    def edge(begin, free, some, block):
        row = begin % rows + lax.broadcasted_iota(jnp.int32, (sub, some - free), 0)
        query_pos = row // part * owned + offset + row % part
        key_pos = free + lax.broadcasted_iota(jnp.int32, (sub, some - free), 1)
        return jnp.where(key_pos <= query_pos, block, MASKED)

    def peak(causal, pair, quarter):
        for at, free, some in blocks(causal, pair, quarter):
            most = jnp.full((sub, 1), MASKED, jnp.float32)
            if free:
                most = jnp.max(s[pair % 3][at, 0:free], axis=-1, keepdims=True)
            if some > free:
                block = edge(at.start, free, some, s[pair % 3][at, free:some])
                most = jnp.maximum(most, jnp.max(block, axis=-1, keepdims=True))
            top[pair % 3, at, :] = jnp.broadcast_to(most, (sub, 128))

    def soften(causal, pair, quarter):
        for at, free, some in blocks(causal, pair, quarter):
            most = top[pair % 3, at, 0:1]
            if free:
                block = s[pair % 3][at, 0:free]
                p[pair % 2, at, 0:free] = jnp.exp2((block - most) * EXP2_SCALE).astype(jnp.bfloat16)
            if some > free:
                block = edge(at.start, free, some, s[pair % 3][at, free:some])
                p[pair % 2, at, free:some] = jnp.exp2((block - most) * EXP2_SCALE).astype(jnp.bfloat16)
            if count > some:
                p[pair % 2, at, some:count] = jnp.zeros((sub, count - some), jnp.bfloat16)

    def blend(pair, half):
        ones = jnp.ones((count, 128), jnp.bfloat16)
        at = slice(half * rows, (half + 1) * rows)
        halves[half] = jnp.dot(
            p[pair % 2, at, :],
            jnp.concatenate([values[:, at_pair(pair)], ones], axis=1),
            preferred_element_type=jnp.float32,
        )

    def close(pair):
        even, odd = halves[0], halves[1]
        both = jnp.where(low, even[:, 0:128], odd[:, 0:128]) / jnp.where(low, even[:, 128:256], odd[:, 128:256])
        out[:, :, at_pair(pair)] = both.astype(jnp.bfloat16).reshape(group, part, 128)
        lane = lax.broadcasted_iota(jnp.int32, (rows, 128), 1)
        held = lse[...]
        for half, mixed in enumerate((even, odd)):
            level = top[pair % 3, half * rows : (half + 1) * rows, :] * EXP2_SCALE + jnp.log2(mixed[:, 128:256])
            held = jnp.where(lane == 2 * pair + half, level, held)
        lse[...] = held

    def attention(causal):
        lse[...] = jnp.zeros_like(lse)
        for turn in range(PAIRS + 3):
            for quarter in range(quarters):
                if turn < PAIRS:
                    score(turn, quarter)
                if 0 <= turn - 3 and quarter % 2 == 0:
                    blend(turn - 3, quarter // 2)
                if 0 <= turn - 2 < PAIRS:
                    soften(causal, turn - 2, quarter)
                if 0 <= turn - 3 and quarter == 3:
                    close(turn - 3)
                if 0 <= turn - 1 < PAIRS:
                    peak(causal, turn - 1, quarter)
        level = lse[...]
        one = level.astype(jnp.bfloat16).astype(jnp.float32)
        two = (level - one).astype(jnp.bfloat16).astype(jnp.float32)
        three = level - one - two
        pieces = one + pltpu.roll(two, HEADS, 1) + pltpu.roll(three, 2 * HEADS, 1)
        out[:, :, D:WIDE] = pieces.astype(jnp.bfloat16).reshape(group, part, 128)

    @pl.when(flag[0] == 0)
    def _():
        attention(False)

    @pl.when(flag[0] != 0)
    def _():
        attention(True)


def attend(first, place, steps, size, owned, is_last, queries, keys, values, into=None):
    group = queries.shape[0]
    rows = group * PART
    count = keys.shape[0]
    whole = lambda c: (0, 0)
    aliased = 0 if into is None else 1
    return pl.pallas_call(
        functools.partial(attend_kernel, first, owned, aliased),
        grid=(steps,),
        out_shape=jax.ShapeDtypeStruct((group, size, WIDE), jnp.bfloat16),
        in_specs=[
            pl.BlockSpec(memory_space=pltpu.SMEM),
            pl.BlockSpec((group, PART, D), lambda c: (0, c, 0)),
            pl.BlockSpec((count, D), whole, pipeline_mode=pl.Buffered(1)),
            pl.BlockSpec((count, D), whole, pipeline_mode=pl.Buffered(1)),
        ]
        + [pl.BlockSpec(memory_space=pl.ANY)] * aliased,
        out_specs=pl.BlockSpec((group, PART, WIDE), lambda c: (0, place + c, 0)),
        scratch_shapes=[pltpu.VMEM((2 * rows, count), jnp.float32)] * 3
        + [
            pltpu.VMEM((2, 2 * rows, count), jnp.bfloat16),
            pltpu.VMEM((3, 2 * rows, 128), jnp.float32),
            pltpu.VMEM((2, rows, 256), jnp.float32),
            pltpu.VMEM((rows, 128), jnp.float32),
        ],
        input_output_aliases={4: 0} if aliased else {},
        compiler_params=pltpu.CompilerParams(vmem_limit_bytes=56 * MIB),
        cost_estimate=pl.CostEstimate(
            flops=16 * steps * rows * D * D,
            bytes_accessed=8 * D * D,
            transcendentals=HEADS * steps * rows * D,
        ),
        name="attend_%d" % first,
    )(is_last, queries, keys, values, *([] if into is None else [into]))


def finish_kernel(number, *refs):
    parts, owns = refs[:number], refs[number : number + 2]
    gain, w_out, out = refs[number + 2 :]
    head = lax.broadcasted_iota(jnp.int32, (128, D), 0)
    column = lax.broadcasted_iota(jnp.int32, (128, D), 1)
    spread = (column // HEAD_DIM == head).astype(jnp.bfloat16)
    spread = jnp.concatenate([spread, spread], axis=0)
    posts = []
    for each in parts:
        count, part, _ = each.shape
        lane = lax.broadcasted_iota(jnp.int32, (count * part, 128), 1)
        pieces = each[:, :, D:WIDE].astype(jnp.float32).reshape(count * part, 128)
        level = pieces + pltpu.roll(pieces, 128 - HEADS, 1) + pltpu.roll(pieces, 128 - 2 * HEADS, 1)
        level = jnp.where(lane < HEADS, level, 0.0).reshape(count, part, 128)
        weight = jnp.exp2(level - jnp.max(level, axis=0, keepdims=True))
        weight = weight / jnp.sum(weight, axis=0, keepdims=True)
        weight = weight.reshape(count * part, 128)
        high = weight.astype(jnp.bfloat16)
        rest = (weight - high.astype(jnp.float32)).astype(jnp.bfloat16)
        wide = jnp.dot(
            jnp.concatenate([high, rest], axis=1), spread, preferred_element_type=jnp.float32
        ).reshape(count, part, D)
        mix = jnp.sum(wide * each[:, :, 0:D].astype(jnp.float32), axis=0)
        posts.append(rms_rows(mix.astype(jnp.bfloat16), gain[...]))
    own = jnp.concatenate([rows[...] for rows in owns], axis=0)
    mixed = own.astype(jnp.float32) + jnp.dot(
        jnp.concatenate(posts, axis=0), w_out[...], preferred_element_type=jnp.float32
    )
    out[...] = mixed.astype(jnp.bfloat16)


def finish(parts, owns, gain, w_out):
    rows = sum(own.shape[0] for own in owns)
    return pl.pallas_call(
        functools.partial(finish_kernel, len(parts)),
        out_shape=jax.ShapeDtypeStruct((rows, D), jnp.bfloat16),
        compiler_params=pltpu.CompilerParams(vmem_limit_bytes=28 * MIB),
        cost_estimate=pl.CostEstimate(flops=4 * rows * D * D, bytes_accessed=8 * D * D, transcendentals=0),
        name="finish",
    )(*parts, *owns, gain, w_out)


def pack_kernel(owned, source, flag, tokens, own, *bundles):
    rows = own.shape[0]

    def block(to):
        return tokens[(to + 1) * owned - rows : (to + 1) * owned, :]

    mine = block(source)
    own[...] = jnp.where(flag[0] != 0, mine, jnp.zeros_like(mine))
    for members, bundle in zip(BUNDLES, bundles):
        for place in range(4):
            at = slice(place * rows, (place + 1) * rows)
            bundle[at, :] = block(members[min(place, len(members) - 1)])


def relay_kernel(*refs):
    bundles, outs = refs[:4], refs[4:]
    rows = outs[0].shape[0]
    for place, out in enumerate(outs):
        at = slice(place * rows, (place + 1) * rows)
        total = bundles[0][at, :].astype(jnp.float32)
        for bundle in bundles[1:]:
            total = total + bundle[at, :].astype(jnp.float32)
        out[...] = total.astype(jnp.bfloat16)


def send_bundles(tokens, owned, rows, source, flag):
    own, *bundles = pl.pallas_call(
        functools.partial(pack_kernel, owned, source),
        out_shape=(jax.ShapeDtypeStruct((rows, D), jnp.bfloat16),)
        + (jax.ShapeDtypeStruct((4 * rows, D), jnp.bfloat16),) * 4,
        in_specs=[pl.BlockSpec(memory_space=pltpu.SMEM), pl.BlockSpec(memory_space=pltpu.VMEM)],
        compiler_params=pltpu.CompilerParams(vmem_limit_bytes=56 * MIB),
        cost_estimate=pl.CostEstimate(flops=0, bytes_accessed=8 * D * D, transcendentals=0),
        name="pack",
    )(flag, tokens)
    bundles = [
        lax.ppermute(bundle, "seq", [(source, members[0])]) for members, bundle in zip(BUNDLES, bundles)
    ]
    return own, bundles


def pass_on(own, bundles):
    kept, *passed = pl.pallas_call(
        relay_kernel,
        out_shape=(jax.ShapeDtypeStruct(own.shape, jnp.bfloat16),) * 4,
        compiler_params=pltpu.CompilerParams(vmem_limit_bytes=24 * MIB),
        cost_estimate=pl.CostEstimate(flops=0, bytes_accessed=4 * D * D, transcendentals=0),
        name="relay",
    )(*bundles)
    parts = [own, kept]
    for place in range(1, 4):
        pairs = [(members[0], members[place]) for members in BUNDLES if place < len(members)]
        parts.append(lax.ppermute(passed[place - 1], "seq", pairs))
    return parts


def after(value, *others):
    return lax.optimization_barrier((value, others))[0]


def local(tokens, ln_gain, post_gain, w_query, w_key, w_value, w_out):
    count = lax.axis_size("seq")
    last = lax.axis_index("seq") == count - 1
    flag = last.astype(jnp.int32).reshape(1)
    owned = LATENTS // count
    gain = ln_gain.reshape(1, D)
    exchange = lambda blocks: lax.all_to_all(blocks, "seq", 0, 0)

    blocks = tokens.reshape(count, owned, D)[:, :PART]
    own_late, bundles = send_bundles(after(tokens, blocks), owned, owned - PART, count - 1, flag)
    keys = project(after(tokens, own_late), gain, w_key, "project_keys")
    scattered = exchange(blocks)
    own_first, tiled_0 = project_queries(count, gain, w_query, [after(scattered, keys)], (PART,))
    rows_0 = exchange(tiled_0)
    parts = pass_on(own_late, after(bundles, tiled_0))
    values = project(after(tokens, parts[1]), gain, w_value, "project_values")
    own_late, tiled_1, tiled_2 = project_queries(
        count, gain, w_query, after(parts, values), (PART, owned - 2 * PART)
    )
    rows_0, tiled_1 = lax.optimization_barrier((rows_0, tiled_1))
    rows_1 = exchange(tiled_1)
    mixed_0 = attend(0, 0, 1, 2 * PART, owned, flag, rows_0, keys, values)
    rows_1, tiled_2, mixed_0 = lax.optimization_barrier((rows_1, tiled_2, mixed_0))
    rows_2 = exchange(tiled_2)
    mixed_0 = attend(1, 1, 1, 2 * PART, owned, flag, rows_1, keys, values, mixed_0)
    rows_2, mixed_0 = lax.optimization_barrier((rows_2, mixed_0))
    mixed_0 = exchange(mixed_0)
    mixed_1 = exchange(attend(2, 0, 2, 2 * PART, owned, flag, rows_2, keys, values))
    return finish((mixed_0, mixed_1), (own_first, own_late), post_gain.reshape(1, D), w_out)


def solution(mesh):
    return jax.shard_map(
        local,
        mesh=mesh,
        in_specs=(P(("ctx", "seq"), None), P(), P(), P(), P(), P(), P()),
        out_specs=P(("ctx", "seq"), None),
        check_vma=False,
    )
```

```python
import functools

import jax
import jax.numpy as jnp
from jax import lax
from jax.experimental import pallas as pl
from jax.experimental.pallas import tpu as pltpu
from jax.sharding import PartitionSpec as P

D = 1024
HEADS = 16
HEAD_DIM = 64
LATENTS = 1024
LOG2E = 1.4426950408889634
EXP2_SCALE = LOG2E * HEAD_DIM ** (-0.5)
MASKED = -1e30
MIB = 2**20
SMEM = pl.BlockSpec(memory_space=pltpu.SMEM)
VMEM = pl.BlockSpec(memory_space=pltpu.VMEM)

BUNDLES = ((3, 0, 2, 1), (11, 8, 10, 9), (12, 13, 4, 5), (14, 6, 7))


def limit(mib):
    return pltpu.CompilerParams(vmem_limit_bytes=mib * MIB)


def low_lanes():
    return lax.broadcasted_iota(jnp.int32, (1, 128), 1) < HEAD_DIM


def rms_rows(rows, gain):
    wide = rows.astype(jnp.float32)
    scale = lax.rsqrt(jnp.mean(wide * wide, axis=-1, keepdims=True) + 1e-06)
    return (wide * scale * gain).astype(jnp.bfloat16)


def kv_kernel(tokens, gain, w_key, w_value, out, normed):
    @pl.when(pl.program_id(0) == 0)
    def _():
        normed[...] = rms_rows(tokens[...], gain[...])

    rows = normed[...]
    keys = jnp.dot(rows, w_key[...], preferred_element_type=jnp.float32)
    values = jnp.dot(rows, w_value[...], preferred_element_type=jnp.float32)
    low = low_lanes()
    for pair in range(out.shape[0] // 2):
        at = slice(pair * 128, (pair + 1) * 128)
        key, value = keys[:, at], values[:, at]
        out[2 * pair] = jnp.where(low, key, pltpu.roll(value, HEAD_DIM, 1)).astype(jnp.bfloat16)
        out[2 * pair + 1] = jnp.where(low, pltpu.roll(key, HEAD_DIM, 1), value).astype(jnp.bfloat16)


def project_kv(tokens, part, parts, gain, w_key, w_value):
    rows = tokens.shape[0] // parts
    cols = 256
    heads = cols // HEAD_DIM
    return pl.pallas_call(
        kv_kernel,
        grid=(D // cols,),
        out_shape=jax.ShapeDtypeStruct((HEADS, rows, 128), jnp.bfloat16),
        in_specs=[
            pl.BlockSpec((rows, D), lambda c: (part, 0)),
            pl.BlockSpec((1, D), lambda c: (0, 0)),
            pl.BlockSpec((D, cols), lambda c: (0, c)),
            pl.BlockSpec((D, cols), lambda c: (0, c)),
        ],
        out_specs=pl.BlockSpec((heads, rows, 128), lambda c: (c, 0, 0)),
        scratch_shapes=[pltpu.VMEM((rows, D), jnp.bfloat16)],
        compiler_params=limit(56),
        cost_estimate=pl.CostEstimate(flops=4 * rows * D * D, bytes_accessed=4 * D * D, transcendentals=0),
        name="project_kv_%d" % part,
    )(tokens, gain, w_key, w_value)


def query_kernel(source, flag, tokens, gain, w_query, own, *bundles):
    queries = jnp.dot(
        rms_rows(tokens[...], gain[...]), w_query[...], preferred_element_type=jnp.float32
    )
    rows = queries.shape[0] // 2
    low = low_lanes()

    def head(number):
        at = slice(number // 2 * 128, (number // 2 + 1) * 128)
        first, second = queries[:rows, at], queries[rows:, at]
        if number % 2:
            first = pltpu.roll(first, HEAD_DIM, 1)
        else:
            second = pltpu.roll(second, HEAD_DIM, 1)
        return jnp.where(low, first, second).astype(jnp.bfloat16)

    mine = head(source)
    own[...] = jnp.where(flag[0] != 0, mine, jnp.zeros_like(mine))
    for members, bundle in zip(BUNDLES, bundles):
        for place in range(4):
            bundle[place] = head(members[min(place, len(members) - 1)])


def project_queries(flag, tokens, gain, w_query, source):
    rows = tokens.shape[0] // 2
    return pl.pallas_call(
        functools.partial(query_kernel, source),
        out_shape=(jax.ShapeDtypeStruct((rows, 128), jnp.bfloat16),)
        + (jax.ShapeDtypeStruct((4, rows, 128), jnp.bfloat16),) * 4,
        in_specs=[SMEM, VMEM, VMEM, VMEM],
        compiler_params=limit(56),
        cost_estimate=pl.CostEstimate(flops=4 * rows * D * D, bytes_accessed=8 * rows * D, transcendentals=0),
        name="project_queries",
    )(flag, tokens, gain, w_query)


def pack_kernel(source, flag, tokens, own, *bundles):
    rows = own.shape[0]

    def block(to):
        return tokens[to * rows : (to + 1) * rows, :]

    mine = block(source)
    own[...] = jnp.where(flag[0] != 0, mine, jnp.zeros_like(mine))
    for members, bundle in zip(BUNDLES, bundles):
        for place in range(4):
            bundle[place] = block(members[min(place, len(members) - 1)])


def pack_rows(flag, tokens, owned, source):
    return pl.pallas_call(
        functools.partial(pack_kernel, source),
        out_shape=(jax.ShapeDtypeStruct((owned, D), jnp.bfloat16),)
        + (jax.ShapeDtypeStruct((4, owned, D), jnp.bfloat16),) * 4,
        in_specs=[SMEM, VMEM],
        compiler_params=limit(56),
        cost_estimate=pl.CostEstimate(flops=0, bytes_accessed=8 * D * D, transcendentals=0),
        name="pack_rows",
    )(flag, tokens)


def relay_kernel(*refs):
    bundles, outs = refs[:4], refs[4:]
    for place, out in enumerate(outs):
        total = bundles[0][place].astype(jnp.float32)
        for bundle in bundles[1:]:
            total = total + bundle[place].astype(jnp.float32)
        out[...] = total.astype(jnp.bfloat16)


def send_bundles(bundles, source):
    return [lax.ppermute(bundle, "seq", [(source, members[0])]) for members, bundle in zip(BUNDLES, bundles)]


def pass_on(own, bundles):
    kept, *passed = pl.pallas_call(
        relay_kernel,
        out_shape=(jax.ShapeDtypeStruct(own.shape, jnp.bfloat16),) * 4,
        compiler_params=limit(24),
        cost_estimate=pl.CostEstimate(flops=0, bytes_accessed=4 * D * D, transcendentals=0),
        name="relay",
    )(*bundles)
    parts = [own, kept]
    for place in range(1, 4):
        pairs = [(members[0], members[place]) for members in BUNDLES if place < len(members)]
        parts.append(lax.ppermute(passed[place - 1], "seq", pairs))
    return parts


def add_parts(parts):
    total = parts[0][...].astype(jnp.float32)
    for part in parts[1:]:
        total = total + part[...].astype(jnp.float32)
    return total


def attend_kernel(base, final, *refs):
    parts, refs = refs[:5], refs[5:]
    kv, refs = refs[0], refs[1:]
    if final:
        acc_in, run_in, out, *refs = refs
        s, p, top, alpha, queries, acc, run = refs[:3], *refs[3:]
    else:
        acc, run, *refs = refs
        s, p, top, alpha, queries = refs[:3], *refs[3:]
    devices, span, _ = kv.shape
    rows = parts[0].shape[0]
    count = 2 * span
    units = devices
    sub = 32
    quarters = 4
    low = low_lanes()

    def keys_of(unit):
        return kv[unit // 2 * 2 : unit // 2 * 2 + 2].reshape(count, 128)

    def score(unit, quarter):
        width = count // quarters
        at = slice(quarter * width, (quarter + 1) * width)
        s[unit % 3][:, at] = lax.dot_general(
            queries[unit % 2],
            keys_of(unit)[at],
            (((1,), (1,)), ((), ())),
            preferred_element_type=jnp.float32,
        )

    def blocks(unit, quarter):
        height = rows // quarters
        for begin in range(quarter * height, (quarter + 1) * height, sub):
            free = some = count
            if unit // 2 * 2 + 2 == devices:
                row = unit % 2 * rows + begin - base
                free = span + min(span, max(0, (row + 1) // 128 * 128))
                some = span + min(span, max(0, -(-(row + sub) // 128) * 128))
            yield slice(begin, begin + sub), free, some

    def edge(unit, begin, free, some, block):
        row = unit % 2 * rows + begin - base + lax.broadcasted_iota(jnp.int32, (sub, some - free), 0)
        key = free - span + lax.broadcasted_iota(jnp.int32, (sub, some - free), 1)
        return jnp.where(key <= row, block, MASKED)

    def peak(unit, quarter):
        for at, free, some in blocks(unit, quarter):
            most = jnp.max(s[unit % 3][at, 0:free], axis=-1, keepdims=True)
            if some > free:
                block = edge(unit, at.start, free, some, s[unit % 3][at, free:some])
                most = jnp.maximum(most, jnp.max(block, axis=-1, keepdims=True))
            before = run[unit % 2, at, :]
            most = jnp.maximum(before, most)
            alpha[unit % 3, at, :] = jnp.exp2((before - most) * EXP2_SCALE)
            run[unit % 2, at, :] = most
            top[unit % 2, at, :] = most

    def soften(unit, quarter):
        for at, free, some in blocks(unit, quarter):
            most = top[unit % 2, at, 0:1]
            block = s[unit % 3][at, 0:free]
            p[unit % 2, at, 0:free] = jnp.exp2((block - most) * EXP2_SCALE).astype(jnp.bfloat16)
            if some > free:
                block = edge(unit, at.start, free, some, s[unit % 3][at, free:some])
                p[unit % 2, at, free:some] = jnp.exp2((block - most) * EXP2_SCALE).astype(jnp.bfloat16)
            if count > some:
                p[unit % 2, at, some:count] = jnp.zeros((sub, count - some), jnp.bfloat16)

    def blend(unit, half):
        height = rows // 2
        at = slice(half * height, (half + 1) * height)
        ones = jnp.ones((count, 128), jnp.bfloat16)
        mixed = jnp.dot(
            p[unit % 2, at, :],
            jnp.concatenate([keys_of(unit), ones], axis=1),
            preferred_element_type=jnp.float32,
        )
        scale = alpha[unit % 3, at, :]
        acc[unit % 2, at, 0:128] = acc[unit % 2, at, 0:128] * scale + mixed[:, 0:128]
        acc[unit % 2, at, 128:256] = acc[unit % 2, at, 128:256] * scale + mixed[:, 128:256]

    both = add_parts(parts)
    none = jnp.zeros_like(both)
    queries[0] = jnp.where(low, both, none).astype(jnp.bfloat16)
    queries[1] = jnp.where(low, pltpu.roll(both, HEAD_DIM, 1), none).astype(jnp.bfloat16)
    if final:
        acc[...] = acc_in[...]
        run[...] = run_in[...]
    else:
        acc[...] = jnp.zeros_like(acc)
        run[...] = jnp.full(run.shape, MASKED, jnp.float32)
    for turn in range(units + 3):
        for quarter in range(quarters):
            if turn < units:
                score(turn, quarter)
            if 0 <= turn - 3 and quarter % 2 == 0:
                blend(turn - 3, quarter // 2)
            if 0 <= turn - 2 < units:
                soften(turn - 2, quarter)
            if 0 <= turn - 1 < units:
                peak(turn - 1, quarter)
    if final:
        for half in range(2):
            at = slice(half * rows, (half + 1) * rows)
            out[at, :] = (acc[half, :, 0:128] / acc[half, :, 128:256]).astype(jnp.bfloat16)


def attend(base, parts, kv, state=None):
    devices, span, _ = kv.shape
    rows = parts[0].shape[0]
    final = state is not None
    acc = (2, rows, 256)
    run = (2, rows, 128)
    shapes = (jax.ShapeDtypeStruct(acc, jnp.float32), jax.ShapeDtypeStruct(run, jnp.float32))
    return pl.pallas_call(
        functools.partial(attend_kernel, base, final),
        out_shape=jax.ShapeDtypeStruct((2 * rows, 128), jnp.bfloat16) if final else shapes,
        scratch_shapes=[pltpu.VMEM((rows, 2 * span), jnp.float32)] * 3
        + [
            pltpu.VMEM((2, rows, 2 * span), jnp.bfloat16),
            pltpu.VMEM(run, jnp.float32),
            pltpu.VMEM((3, rows, 128), jnp.float32),
            pltpu.VMEM((2, rows, 128), jnp.bfloat16),
        ]
        + ([pltpu.VMEM(acc, jnp.float32), pltpu.VMEM(run, jnp.float32)] if final else []),
        compiler_params=limit(56),
        cost_estimate=pl.CostEstimate(
            flops=4 * 256 * 2 * rows * devices * span,
            bytes_accessed=4 * D * D,
            transcendentals=2 * rows * devices * span,
        ),
        name="attend_%d" % base,
    )(*parts, kv, *(state or ()))


def finish_kernel(heads, *refs):
    parts, (gain, w_out, out) = refs[:5], refs[5:]
    low = low_lanes()
    pairs = []
    for pair in range(HEADS // 2):
        even, odd = heads[2 * pair].astype(jnp.float32), heads[2 * pair + 1].astype(jnp.float32)
        pairs.append(jnp.where(low, pltpu.roll(even, HEAD_DIM, 1), odd))
    attended = jnp.concatenate(pairs, axis=1).astype(jnp.bfloat16)
    post = rms_rows(attended, gain[...])
    mixed = add_parts(parts) + jnp.dot(post, w_out[...], preferred_element_type=jnp.float32)
    out[...] = mixed.astype(jnp.bfloat16)


def finish(heads, parts, gain, w_out):
    rows = heads.shape[1]
    return pl.pallas_call(
        finish_kernel,
        out_shape=jax.ShapeDtypeStruct((rows, D), jnp.bfloat16),
        compiler_params=limit(28),
        cost_estimate=pl.CostEstimate(flops=2 * rows * D * D, bytes_accessed=4 * D * D, transcendentals=0),
        name="finish",
    )(heads, *parts, gain, w_out)


def after(value, *others):
    return lax.optimization_barrier((value, others))[0]


def local(tokens, ln_gain, post_gain, w_query, w_key, w_value, w_out):
    count = lax.axis_size("seq")
    source = count - 1
    last = lax.axis_index("seq") == source
    flag = last.astype(jnp.int32).reshape(1)
    owned = LATENTS // count
    gain = ln_gain.reshape(1, D)
    exchange = lambda blocks: lax.all_to_all(blocks, "seq", 0, 0)

    kv_0 = project_kv(tokens, 0, 2, gain, w_key, w_value)
    sent_0 = exchange(kv_0)
    own, *bundles = project_queries(flag, after(tokens, kv_0), gain, w_query, source)
    came = send_bundles(bundles, source)
    kv_1 = project_kv(after(tokens, bundles), 1, 2, gain, w_key, w_value)
    queries = pass_on(own, after(came, kv_1))
    own, *bundles = pack_rows(flag, after(tokens, queries[1]), owned, source)
    came = send_bundles(bundles, source)
    sent_0, kv_1 = lax.optimization_barrier((sent_0, kv_1))
    sent_1 = exchange(kv_1)
    state = attend(0, queries, sent_0)
    rows = pass_on(own, after(came, state))
    mixed = attend(tokens.shape[0] // 2, queries, after(sent_1, state, rows[1]), state)
    heads = exchange(mixed.reshape(count, owned, 128))
    return finish(heads, rows, post_gain.reshape(1, D), w_out)


def solution(mesh):
    return jax.shard_map(
        local,
        mesh=mesh,
        in_specs=(P(("ctx", "seq"), None), P(), P(), P(), P(), P(), P()),
        out_specs=P(("ctx", "seq"), None),
        check_vma=False,
    )
```

```python
import functools

import jax
import jax.numpy as jnp
from jax import lax
from jax.experimental import pallas as pl
from jax.experimental.pallas import tpu as pltpu
from jax.sharding import PartitionSpec as P

D = 1024
HEADS = 16
HEAD_DIM = 64
PAIRS = HEADS // 2
LATENTS = 1024
PART = 32
LOG2E = 1.4426950408889634
EXP2_SCALE = LOG2E * HEAD_DIM ** (-0.5)
MASKED = -1e30
WIDE = D + 128
MIB = 2**20

BUNDLES = ((3, 0, 2, 1), (11, 8, 10, 9), (12, 13, 4, 5), (14, 6, 7))


def rms_rows(rows, gain):
    wide = rows.astype(jnp.float32)
    scale = lax.rsqrt(jnp.mean(wide * wide, axis=-1, keepdims=True) + 1e-06)
    return (wide * scale * gain).astype(jnp.bfloat16)


def kv_kernel(tokens, gain, w_key, w_value, keys, values, normed):
    @pl.when(pl.program_id(0) == 0)
    def _():
        normed[...] = rms_rows(tokens[...], gain[...])

    rows = normed[...]
    keys[...] = jnp.dot(rows, w_key[...], preferred_element_type=jnp.float32).astype(jnp.bfloat16)
    values[...] = jnp.dot(rows, w_value[...], preferred_element_type=jnp.float32).astype(jnp.bfloat16)


def project_kv(tokens, gain, w_key, w_value):
    rows = tokens.shape[0]
    cols = 256
    whole = lambda c: (0, 0)
    block = lambda c: (0, c)
    return pl.pallas_call(
        kv_kernel,
        grid=(D // cols,),
        out_shape=(jax.ShapeDtypeStruct((rows, D), jnp.bfloat16),) * 2,
        in_specs=[
            pl.BlockSpec((rows, D), whole, pipeline_mode=pl.Buffered(1)),
            pl.BlockSpec((1, D), whole),
            pl.BlockSpec((D, cols), block),
            pl.BlockSpec((D, cols), block),
        ],
        out_specs=(pl.BlockSpec((rows, cols), block),) * 2,
        scratch_shapes=[pltpu.VMEM((rows, D), jnp.bfloat16)],
        compiler_params=pltpu.CompilerParams(vmem_limit_bytes=56 * MIB),
        cost_estimate=pl.CostEstimate(flops=4 * rows * D * D, bytes_accessed=10 * rows * D, transcendentals=0),
        name="project_kv",
    )(tokens, gain, w_key, w_value)


def query_kernel(count, gain, w_query, *refs):
    parts, (own, *tiled) = refs[:5], refs[5:]
    rows = parts[0][...].astype(jnp.float32)
    for part in parts[1:]:
        rows = rows + part[...].astype(jnp.float32)
    rows = rows.astype(jnp.bfloat16)
    own[...] = rows
    queries = jnp.dot(
        rms_rows(rows, gain[...]), w_query[...], preferred_element_type=jnp.float32
    ).astype(jnp.bfloat16)
    begin = 0
    for each in tiled:
        end = begin + each.shape[1]
        for to in range(count):
            each[to] = queries[begin:end]
        begin = end


def project_queries(count, gain, w_query, parts):
    rows = parts[0].shape[0]
    return pl.pallas_call(
        functools.partial(query_kernel, count),
        out_shape=(jax.ShapeDtypeStruct((rows, D), jnp.bfloat16),)
        + tuple(jax.ShapeDtypeStruct((count, each, D), jnp.bfloat16) for each in (PART, rows - PART)),
        compiler_params=pltpu.CompilerParams(vmem_limit_bytes=16 * MIB),
        cost_estimate=pl.CostEstimate(flops=2 * rows * D * D, bytes_accessed=4 * D * D, transcendentals=0),
        name="project_queries",
    )(gain, w_query, *parts)


def attend_kernel(chunk, owned, flag, queries, keys, values, out):
    rows = queries.shape[0]
    count = keys.shape[0]
    step = pl.program_id(0)
    pairs = HEADS // 2
    part = PART
    low = lax.broadcasted_iota(jnp.int32, (1, 128), 1) < HEAD_DIM

    def attention(causal, count):
        lane = lax.broadcasted_iota(jnp.int32, (rows, 128), 1)
        lse = jnp.zeros((rows, 128), jnp.float32)
        ones = jnp.ones((count, 128), jnp.bfloat16)
        if causal:
            key_pos = lax.broadcasted_iota(jnp.int32, (rows, count), 1)
            row = step * rows + lax.broadcasted_iota(jnp.int32, (rows, count), 0)
            query_pos = (row // part) * owned + chunk * part + row % part
            allowed = key_pos <= query_pos
            allowed = jnp.concatenate([allowed, allowed], axis=0)

        def scores_of(pair):
            at = slice(pair * 128, (pair + 1) * 128)
            query = queries[:, at]
            none = jnp.zeros_like(query)
            both = jnp.concatenate([jnp.where(low, query, none), jnp.where(low, none, query)], axis=0)
            scores = lax.dot_general(
                both, keys[0:count, at], (((1,), (1,)), ((), ())), preferred_element_type=jnp.float32
            )
            return jnp.where(allowed, scores, MASKED) if causal else scores

        ahead = scores_of(0)
        for pair in range(pairs):
            at = slice(pair * 128, (pair + 1) * 128)
            scores = ahead
            if pair + 1 < pairs:
                ahead = scores_of(pair + 1)
            top = jnp.max(scores, axis=-1, keepdims=True)
            weights = jnp.exp2((scores - top) * EXP2_SCALE).astype(jnp.bfloat16)
            mixed = jnp.dot(
                weights,
                jnp.concatenate([values[0:count, at], ones], axis=1),
                preferred_element_type=jnp.float32,
            )
            mix, total = mixed[:, 0:128], mixed[:, 128:256]
            both = jnp.where(low, mix[:rows], mix[rows:]) / jnp.where(low, total[:rows], total[rows:])
            out[:, at] = both.astype(jnp.bfloat16)
            level = top * EXP2_SCALE + jnp.log2(total)
            lse = jnp.where(lane == 2 * pair, level[:rows], lse)
            lse = jnp.where(lane == 2 * pair + 1, level[rows:], lse)
        first = lse.astype(jnp.bfloat16).astype(jnp.float32)
        second = (lse - first).astype(jnp.bfloat16).astype(jnp.float32)
        third = lse - first - second
        pieces = first + pltpu.roll(second, HEADS, 1) + pltpu.roll(third, 2 * HEADS, 1)
        out[:, D:WIDE] = pieces.astype(jnp.bfloat16)

    @pl.when(flag[0] == 0)
    def _():
        attention(False, count)

    @pl.when(jnp.logical_and(flag[0] != 0, step == 0))
    def _():
        attention(True, rows // part * owned)

    @pl.when(jnp.logical_and(flag[0] != 0, step != 0))
    def _():
        attention(True, count)


def attend(chunk, owned, is_last, queries, keys, values):
    count = queries.shape[0]
    rows = 256
    whole = lambda c: (0, 0)
    block = lambda c: (c, 0)
    return pl.pallas_call(
        functools.partial(attend_kernel, chunk, owned),
        grid=(count // rows,),
        out_shape=jax.ShapeDtypeStruct((count, WIDE), jnp.bfloat16),
        in_specs=[
            pl.BlockSpec(memory_space=pltpu.SMEM),
            pl.BlockSpec((rows, D), block),
            pl.BlockSpec(keys.shape, whole),
            pl.BlockSpec(values.shape, whole),
        ],
        out_specs=pl.BlockSpec((rows, WIDE), block),
        compiler_params=pltpu.CompilerParams(vmem_limit_bytes=56 * MIB),
        cost_estimate=pl.CostEstimate(
            flops=16 * count * D * D, bytes_accessed=8 * D * D, transcendentals=HEADS * count * D
        ),
        name="attend_%d" % chunk,
    )(is_last, queries, keys, values)


def finish_kernel(number, *refs):
    parts, (own, gain, w_out, out) = refs[:number], refs[number:]
    head = lax.broadcasted_iota(jnp.int32, (128, D), 0)
    column = lax.broadcasted_iota(jnp.int32, (128, D), 1)
    spread = (column // HEAD_DIM == head).astype(jnp.bfloat16)
    spread = jnp.concatenate([spread, spread], axis=0)
    posts = []
    for each in parts:
        count, part, _ = each.shape
        lane = lax.broadcasted_iota(jnp.int32, (count * part, 128), 1)
        pieces = each[:, :, D:WIDE].astype(jnp.float32).reshape(count * part, 128)
        level = pieces + pltpu.roll(pieces, 128 - HEADS, 1) + pltpu.roll(pieces, 128 - 2 * HEADS, 1)
        level = jnp.where(lane < HEADS, level, 0.0).reshape(count, part, 128)
        weight = jnp.exp2(level - jnp.max(level, axis=0, keepdims=True))
        weight = weight / jnp.sum(weight, axis=0, keepdims=True)
        weight = weight.reshape(count * part, 128)
        high = weight.astype(jnp.bfloat16)
        rest = (weight - high.astype(jnp.float32)).astype(jnp.bfloat16)
        wide = jnp.dot(
            jnp.concatenate([high, rest], axis=1), spread, preferred_element_type=jnp.float32
        ).reshape(count, part, D)
        mix = jnp.sum(wide * each[:, :, 0:D].astype(jnp.float32), axis=0)
        posts.append(rms_rows(mix.astype(jnp.bfloat16), gain[...]))
    mixed = own[...].astype(jnp.float32) + jnp.dot(
        jnp.concatenate(posts, axis=0), w_out[...], preferred_element_type=jnp.float32
    )
    out[...] = mixed.astype(jnp.bfloat16)


def finish(parts, own, gain, w_out):
    rows = own.shape[0]
    return pl.pallas_call(
        functools.partial(finish_kernel, len(parts)),
        out_shape=jax.ShapeDtypeStruct((rows, D), jnp.bfloat16),
        compiler_params=pltpu.CompilerParams(vmem_limit_bytes=28 * MIB),
        cost_estimate=pl.CostEstimate(flops=4 * rows * D * D, bytes_accessed=8 * D * D, transcendentals=0),
        name="finish",
    )(*parts, own, gain, w_out)


def pack_kernel(owned, source, flag, tokens, own, *bundles):
    def block(to):
        return tokens[to * owned : (to + 1) * owned, :]

    mine = block(source)
    own[...] = jnp.where(flag[0] != 0, mine, jnp.zeros_like(mine))
    for members, bundle in zip(BUNDLES, bundles):
        for place in range(4):
            at = slice(place * owned, (place + 1) * owned)
            bundle[at, :] = block(members[min(place, len(members) - 1)])


def relay_kernel(*refs):
    bundles, outs = refs[:4], refs[4:]
    rows = outs[0].shape[0]
    for place, out in enumerate(outs):
        at = slice(place * rows, (place + 1) * rows)
        total = bundles[0][at, :].astype(jnp.float32)
        for bundle in bundles[1:]:
            total = total + bundle[at, :].astype(jnp.float32)
        out[...] = total.astype(jnp.bfloat16)


def scatter(tokens, owned, source, flag, beside):
    limit = pltpu.CompilerParams(vmem_limit_bytes=16 * MIB)
    block = jax.ShapeDtypeStruct((owned, D), jnp.bfloat16)
    smem = pl.BlockSpec(memory_space=pltpu.SMEM)
    vmem = pl.BlockSpec(memory_space=pltpu.VMEM)
    own, *bundles = pl.pallas_call(
        functools.partial(pack_kernel, owned, source),
        out_shape=(block,) + (jax.ShapeDtypeStruct((4 * owned, D), jnp.bfloat16),) * 4,
        in_specs=[smem, vmem],
        compiler_params=limit,
        cost_estimate=pl.CostEstimate(flops=0, bytes_accessed=8 * D * D, transcendentals=0),
        name="pack",
    )(flag, tokens)
    bundles = [
        lax.ppermute(bundle, "seq", [(source, members[0])]) for members, bundle in zip(BUNDLES, bundles)
    ]
    bundles, _ = lax.optimization_barrier((bundles, beside))
    kept, *passed = pl.pallas_call(
        relay_kernel,
        out_shape=(block,) * 4,
        compiler_params=limit,
        cost_estimate=pl.CostEstimate(flops=0, bytes_accessed=4 * D * D, transcendentals=0),
        name="relay",
    )(*bundles)
    parts = [own, kept]
    for place in range(1, 4):
        pairs = [(members[0], members[place]) for members in BUNDLES if place < len(members)]
        parts.append(lax.ppermute(passed[place - 1], "seq", pairs))
    return parts


def local(tokens, ln_gain, post_gain, w_query, w_key, w_value, w_out):
    count = lax.axis_size("seq")
    last = lax.axis_index("seq") == count - 1
    flag = last.astype(jnp.int32).reshape(1)
    owned = LATENTS // count
    gain = ln_gain.reshape(1, D)
    keys, values = project_kv(tokens, gain, w_key, w_value)
    parts = scatter(tokens, owned, count - 1, flag, keys)
    own, tiled_a, tiled_b = project_queries(count, gain, w_query, parts)
    rows_a = lax.all_to_all(tiled_a, "seq", 0, 0)
    rows_a, tiled_b = lax.optimization_barrier((rows_a, tiled_b))
    rows_b = lax.all_to_all(tiled_b, "seq", 0, 0)
    mixed_a = attend(0, owned, flag, rows_a.reshape(-1, D), keys, values)
    rows_b, _ = lax.optimization_barrier((rows_b, mixed_a))
    mixed_b = attend(1, owned, flag, rows_b.reshape(-1, D), keys, values)
    mixed = [lax.all_to_all(each.reshape(count, PART, WIDE), "seq", 0, 0) for each in (mixed_a, mixed_b)]
    return finish(mixed, own, post_gain.reshape(1, D), w_out)


def solution(mesh):
    return jax.shard_map(
        local,
        mesh=mesh,
        in_specs=(P(("ctx", "seq"), None), P(), P(), P(), P(), P(), P()),
        out_specs=P(("ctx", "seq"), None),
        check_vma=False,
    )
```

```python
import functools

import jax
import jax.numpy as jnp
from jax import lax
from jax.experimental import pallas as pl
from jax.experimental.pallas import tpu as pltpu
from jax.sharding import PartitionSpec as P

D = 1024
HEADS = 16
HEAD_DIM = 64
PAIRS = HEADS // 2
LATENTS = 1024
PART = 32
LOG2E = 1.4426950408889634
EXP2_SCALE = LOG2E * HEAD_DIM ** (-0.5)
MASKED = -1e30
WIDE = D + 128
MIB = 2**20

BUNDLES = ((3, 0, 2, 1), (11, 8, 10, 9), (12, 13, 4, 5), (14, 6, 7))


def rms_rows(rows, gain):
    wide = rows.astype(jnp.float32)
    scale = lax.rsqrt(jnp.mean(wide * wide, axis=-1, keepdims=True) + 1e-06)
    return (wide * scale * gain).astype(jnp.bfloat16)


def kv_kernel(tokens, gain, w_key, w_value, keys, values, normed):
    @pl.when(pl.program_id(0) == 0)
    def _():
        normed[...] = rms_rows(tokens[...], gain[...])

    rows = normed[...]
    keys[...] = jnp.dot(rows, w_key[...], preferred_element_type=jnp.float32).astype(jnp.bfloat16)
    values[...] = jnp.dot(rows, w_value[...], preferred_element_type=jnp.float32).astype(jnp.bfloat16)


def project_kv(tokens, gain, w_key, w_value):
    rows = tokens.shape[0]
    cols = 256
    whole = lambda c: (0, 0)
    block = lambda c: (0, c)
    return pl.pallas_call(
        kv_kernel,
        grid=(D // cols,),
        out_shape=(jax.ShapeDtypeStruct((rows, D), jnp.bfloat16),) * 2,
        in_specs=[
            pl.BlockSpec((rows, D), whole, pipeline_mode=pl.Buffered(1)),
            pl.BlockSpec((1, D), whole),
            pl.BlockSpec((D, cols), block),
            pl.BlockSpec((D, cols), block),
        ],
        out_specs=(pl.BlockSpec((rows, cols), block),) * 2,
        scratch_shapes=[pltpu.VMEM((rows, D), jnp.bfloat16)],
        compiler_params=pltpu.CompilerParams(vmem_limit_bytes=56 * MIB),
        cost_estimate=pl.CostEstimate(flops=4 * rows * D * D, bytes_accessed=10 * rows * D, transcendentals=0),
        name="project_kv",
    )(tokens, gain, w_key, w_value)


def query_kernel(gain, w_query, *refs):
    parts, (own, tiled) = refs[:5], refs[5:]
    rows = parts[0][...].astype(jnp.float32)
    for part in parts[1:]:
        rows = rows + part[...].astype(jnp.float32)
    rows = rows.astype(jnp.bfloat16)
    own[...] = rows
    queries = jnp.dot(
        rms_rows(rows, gain[...]), w_query[...], preferred_element_type=jnp.float32
    ).astype(jnp.bfloat16)
    for to in range(tiled.shape[0]):
        tiled[to] = queries


def project_queries(count, gain, w_query, parts):
    rows = parts[0].shape[0]
    return pl.pallas_call(
        query_kernel,
        out_shape=(
            jax.ShapeDtypeStruct((rows, D), jnp.bfloat16),
            jax.ShapeDtypeStruct((count, rows, D), jnp.bfloat16),
        ),
        compiler_params=pltpu.CompilerParams(vmem_limit_bytes=16 * MIB),
        cost_estimate=pl.CostEstimate(flops=2 * rows * D * D, bytes_accessed=4 * D * D, transcendentals=0),
        name="project_queries",
    )(gain, w_query, *parts)


def attend_kernel(chunk, owned, flag, queries, keys, values, out):
    rows = queries.shape[0]
    count = keys.shape[0]
    step = pl.program_id(0)
    pairs = HEADS // 2
    part = PART
    low = lax.broadcasted_iota(jnp.int32, (1, 128), 1) < HEAD_DIM

    def attention(causal, count):
        lane = lax.broadcasted_iota(jnp.int32, (rows, 128), 1)
        lse = jnp.zeros((rows, 128), jnp.float32)
        if causal:
            key_pos = lax.broadcasted_iota(jnp.int32, (rows, count), 1)
            row = step * rows + lax.broadcasted_iota(jnp.int32, (rows, count), 0)
            query_pos = (row // part) * owned + chunk * part + row % part
            allowed = key_pos <= query_pos
            allowed = jnp.concatenate([allowed, allowed], axis=0)

        def scores_of(pair):
            at = slice(pair * 128, (pair + 1) * 128)
            query = queries[:, at]
            none = jnp.zeros_like(query)
            both = jnp.concatenate([jnp.where(low, query, none), jnp.where(low, none, query)], axis=0)
            scores = lax.dot_general(
                both, keys[0:count, at], (((1,), (1,)), ((), ())), preferred_element_type=jnp.float32
            )
            return jnp.where(allowed, scores, MASKED) if causal else scores

        ahead = scores_of(0)
        for pair in range(pairs):
            at = slice(pair * 128, (pair + 1) * 128)
            scores = ahead
            if pair + 1 < pairs:
                ahead = scores_of(pair + 1)
            top = jnp.max(scores, axis=-1, keepdims=True)
            weights = jnp.exp2((scores - top) * EXP2_SCALE)
            total = jnp.sum(weights, axis=-1, keepdims=True)
            mix = jnp.dot(
                weights.astype(jnp.bfloat16), values[0:count, at], preferred_element_type=jnp.float32
            )
            both = jnp.where(low, mix[:rows], mix[rows:]) / jnp.where(low, total[:rows], total[rows:])
            out[:, at] = both.astype(jnp.bfloat16)
            level = top * EXP2_SCALE + jnp.log2(total)
            lse = jnp.where(lane == 2 * pair, level[:rows], lse)
            lse = jnp.where(lane == 2 * pair + 1, level[rows:], lse)
        first = lse.astype(jnp.bfloat16).astype(jnp.float32)
        second = (lse - first).astype(jnp.bfloat16).astype(jnp.float32)
        third = lse - first - second
        pieces = first + pltpu.roll(second, HEADS, 1) + pltpu.roll(third, 2 * HEADS, 1)
        out[:, D:WIDE] = pieces.astype(jnp.bfloat16)

    @pl.when(flag[0] == 0)
    def _():
        attention(False, count)

    @pl.when(jnp.logical_and(flag[0] != 0, step == 0))
    def _():
        attention(True, rows // part * owned)

    @pl.when(jnp.logical_and(flag[0] != 0, step != 0))
    def _():
        attention(True, count)


def attend(chunk, owned, is_last, queries, keys, values):
    count = queries.shape[0]
    rows = 256
    whole = lambda c: (0, 0)
    block = lambda c: (c, 0)
    return pl.pallas_call(
        functools.partial(attend_kernel, chunk, owned),
        grid=(count // rows,),
        out_shape=jax.ShapeDtypeStruct((count, WIDE), jnp.bfloat16),
        in_specs=[
            pl.BlockSpec(memory_space=pltpu.SMEM),
            pl.BlockSpec((rows, D), block),
            pl.BlockSpec(keys.shape, whole),
            pl.BlockSpec(values.shape, whole),
        ],
        out_specs=pl.BlockSpec((rows, WIDE), block),
        compiler_params=pltpu.CompilerParams(vmem_limit_bytes=56 * MIB),
        cost_estimate=pl.CostEstimate(
            flops=16 * count * D * D, bytes_accessed=8 * D * D, transcendentals=HEADS * count * D
        ),
        name="attend_%d" % chunk,
    )(is_last, queries, keys, values)


def finish_kernel(number, *refs):
    parts, owns = refs[:number], refs[number : number + 2]
    gain, w_out, out = refs[number + 2 :]
    head = lax.broadcasted_iota(jnp.int32, (128, D), 0)
    column = lax.broadcasted_iota(jnp.int32, (128, D), 1)
    spread = (column // HEAD_DIM == head).astype(jnp.bfloat16)
    spread = jnp.concatenate([spread, spread], axis=0)
    posts = []
    for each in parts:
        count, part, _ = each.shape
        lane = lax.broadcasted_iota(jnp.int32, (count * part, 128), 1)
        pieces = each[:, :, D:WIDE].astype(jnp.float32).reshape(count * part, 128)
        level = pieces + pltpu.roll(pieces, 128 - HEADS, 1) + pltpu.roll(pieces, 128 - 2 * HEADS, 1)
        level = jnp.where(lane < HEADS, level, 0.0).reshape(count, part, 128)
        weight = jnp.exp2(level - jnp.max(level, axis=0, keepdims=True))
        weight = weight / jnp.sum(weight, axis=0, keepdims=True)
        weight = weight.reshape(count * part, 128)
        high = weight.astype(jnp.bfloat16)
        rest = (weight - high.astype(jnp.float32)).astype(jnp.bfloat16)
        wide = jnp.dot(
            jnp.concatenate([high, rest], axis=1), spread, preferred_element_type=jnp.float32
        ).reshape(count, part, D)
        mix = jnp.sum(wide * each[:, :, 0:D].astype(jnp.float32), axis=0)
        posts.append(rms_rows(mix.astype(jnp.bfloat16), gain[...]))
    own = jnp.concatenate([rows[...] for rows in owns], axis=0)
    mixed = own.astype(jnp.float32) + jnp.dot(
        jnp.concatenate(posts, axis=0), w_out[...], preferred_element_type=jnp.float32
    )
    out[...] = mixed.astype(jnp.bfloat16)


def finish(parts, owns, gain, w_out):
    rows = sum(own.shape[0] for own in owns)
    return pl.pallas_call(
        functools.partial(finish_kernel, len(parts)),
        out_shape=jax.ShapeDtypeStruct((rows, D), jnp.bfloat16),
        compiler_params=pltpu.CompilerParams(vmem_limit_bytes=28 * MIB),
        cost_estimate=pl.CostEstimate(flops=4 * rows * D * D, bytes_accessed=8 * D * D, transcendentals=0),
        name="finish",
    )(*parts, *owns, gain, w_out)


def pack_kernel(owned, source, flag, tokens, *outs):
    for half, begin in enumerate(range(0, owned, PART)):
        own, *bundles = outs[5 * half : 5 * half + 5]

        def block(to):
            return tokens[to * owned + begin : to * owned + begin + PART, :]

        mine = block(source)
        own[...] = jnp.where(flag[0] != 0, mine, jnp.zeros_like(mine))
        for members, bundle in zip(BUNDLES, bundles):
            for place in range(4):
                at = slice(place * PART, (place + 1) * PART)
                bundle[at, :] = block(members[min(place, len(members) - 1)])


def pack(tokens, owned, source, flag):
    shapes = (jax.ShapeDtypeStruct((PART, D), jnp.bfloat16),)
    shapes += (jax.ShapeDtypeStruct((4 * PART, D), jnp.bfloat16),) * 4
    outs = pl.pallas_call(
        functools.partial(pack_kernel, owned, source),
        out_shape=shapes * (owned // PART),
        in_specs=[pl.BlockSpec(memory_space=pltpu.SMEM), pl.BlockSpec(memory_space=pltpu.VMEM)],
        compiler_params=pltpu.CompilerParams(vmem_limit_bytes=16 * MIB),
        cost_estimate=pl.CostEstimate(flops=0, bytes_accessed=8 * D * D, transcendentals=0),
        name="pack",
    )(flag, tokens)
    return outs[:5], outs[5:]


def send_bundles(bundles, source):
    return [lax.ppermute(bundle, "seq", [(source, members[0])]) for members, bundle in zip(BUNDLES, bundles)]


def relay_kernel(*refs):
    bundles, outs = refs[:4], refs[4:]
    rows = outs[0].shape[0]
    for place, out in enumerate(outs):
        at = slice(place * rows, (place + 1) * rows)
        total = bundles[0][at, :].astype(jnp.float32)
        for bundle in bundles[1:]:
            total = total + bundle[at, :].astype(jnp.float32)
        out[...] = total.astype(jnp.bfloat16)


def pass_on(own, bundles):
    kept, *passed = pl.pallas_call(
        relay_kernel,
        out_shape=(jax.ShapeDtypeStruct(own.shape, jnp.bfloat16),) * 4,
        compiler_params=pltpu.CompilerParams(vmem_limit_bytes=16 * MIB),
        cost_estimate=pl.CostEstimate(flops=0, bytes_accessed=4 * D * D, transcendentals=0),
        name="relay",
    )(*bundles)
    parts = [own, kept]
    for place in range(1, 4):
        pairs = [(members[0], members[place]) for members in BUNDLES if place < len(members)]
        parts.append(lax.ppermute(passed[place - 1], "seq", pairs))
    return parts


def after(value, *others):
    return lax.optimization_barrier((value, others))[0]


def local(tokens, ln_gain, post_gain, w_query, w_key, w_value, w_out):
    count = lax.axis_size("seq")
    source = count - 1
    last = lax.axis_index("seq") == source
    flag = last.astype(jnp.int32).reshape(1)
    owned = LATENTS // count
    gain = ln_gain.reshape(1, D)
    exchange = lambda blocks: lax.all_to_all(blocks, "seq", 0, 0)

    (own_a, *bundles_a), (own_b, *bundles_b) = pack(tokens, owned, source, flag)
    came_a, came_b = send_bundles(bundles_a, source), send_bundles(bundles_b, source)
    own_a, tiled_a = project_queries(count, gain, w_query, pass_on(own_a, came_a))
    rows_a = exchange(tiled_a)
    parts_b = pass_on(own_b, after(came_b, tiled_a))
    keys, values = project_kv(after(tokens, parts_b[1]), gain, w_key, w_value)
    own_b, tiled_b = project_queries(count, gain, w_query, after(parts_b, keys))
    rows_a, tiled_b = lax.optimization_barrier((rows_a, tiled_b))
    rows_b = exchange(tiled_b)
    mixed_a = attend(0, owned, flag, rows_a.reshape(-1, D), keys, values)
    mixed_b = attend(1, owned, flag, after(rows_b, mixed_a).reshape(-1, D), keys, values)
    mixed = [exchange(each.reshape(count, PART, WIDE)) for each in (mixed_a, mixed_b)]
    return finish(mixed, (own_a, own_b), post_gain.reshape(1, D), w_out)


def solution(mesh):
    return jax.shard_map(
        local,
        mesh=mesh,
        in_specs=(P(("ctx", "seq"), None), P(), P(), P(), P(), P(), P()),
        out_specs=P(("ctx", "seq"), None),
        check_vma=False,
    )
```

```python
import functools

import jax
import jax.numpy as jnp
from jax import lax
from jax.experimental import pallas as pl
from jax.experimental.pallas import tpu as pltpu
from jax.sharding import PartitionSpec as P

D = 1024
HEADS = 16
HEAD_DIM = 64
PAIRS = HEADS // 2
LATENTS = 1024
PART = 32
SPLIT = 4
LOG2E = 1.4426950408889634
EXP2_SCALE = LOG2E * HEAD_DIM ** (-0.5)
MASKED = -1e30
WIDE = D + 128
MIB = 2**20

BUNDLES = ((3, 0, 2, 1), (11, 8, 10, 9), (12, 13, 4, 5), (14, 6, 7))


def rms_rows(rows, gain):
    wide = rows.astype(jnp.float32)
    scale = lax.rsqrt(jnp.mean(wide * wide, axis=-1, keepdims=True) + 1e-06)
    return (wide * scale * gain).astype(jnp.bfloat16)


def kv_kernel(tokens, gain, w_key, w_value, keys, values, normed):
    @pl.when(pl.program_id(0) == 0)
    def _():
        normed[...] = rms_rows(tokens[...], gain[...])

    rows = normed[...]
    keys[...] = jnp.dot(rows, w_key[...], preferred_element_type=jnp.float32).T.astype(jnp.bfloat16)
    values[...] = jnp.dot(rows, w_value[...], preferred_element_type=jnp.float32).astype(jnp.bfloat16)


def project_kv(tokens, gain, w_key, w_value):
    rows = tokens.shape[0]
    cols = 256
    whole = lambda c: (0, 0)
    block = lambda c: (0, c)
    return pl.pallas_call(
        kv_kernel,
        grid=(D // cols,),
        out_shape=(
            jax.ShapeDtypeStruct((D, rows), jnp.bfloat16),
            jax.ShapeDtypeStruct((rows, D), jnp.bfloat16),
        ),
        in_specs=[
            pl.BlockSpec((rows, D), whole, pipeline_mode=pl.Buffered(1)),
            pl.BlockSpec((1, D), whole),
            pl.BlockSpec((D, cols), block),
            pl.BlockSpec((D, cols), block),
        ],
        out_specs=(pl.BlockSpec((cols, rows), lambda c: (c, 0)), pl.BlockSpec((rows, cols), block)),
        scratch_shapes=[pltpu.VMEM((rows, D), jnp.bfloat16)],
        compiler_params=pltpu.CompilerParams(vmem_limit_bytes=56 * MIB),
        cost_estimate=pl.CostEstimate(flops=4 * rows * D * D, bytes_accessed=10 * rows * D, transcendentals=0),
        name="project_kv",
    )(tokens, gain, w_key, w_value)


def query_kernel(count, gain, w_query, *refs):
    parts, (own, *tiled) = refs[:5], refs[5:]
    rows = parts[0][...].astype(jnp.float32)
    for part in parts[1:]:
        rows = rows + part[...].astype(jnp.float32)
    rows = rows.astype(jnp.bfloat16)
    own[...] = rows
    queries = jnp.dot(
        rms_rows(rows, gain[...]), w_query[...], preferred_element_type=jnp.float32
    ).astype(jnp.bfloat16)
    begin = 0
    for each in tiled:
        end = begin + each.shape[1]
        for to in range(count):
            each[to] = queries[begin:end]
        begin = end


def project_queries(count, gain, w_query, parts):
    rows = parts[0].shape[0]
    return pl.pallas_call(
        functools.partial(query_kernel, count),
        out_shape=(jax.ShapeDtypeStruct((rows, D), jnp.bfloat16),)
        + tuple(jax.ShapeDtypeStruct((count, each, D), jnp.bfloat16) for each in (PART, rows - PART)),
        compiler_params=pltpu.CompilerParams(vmem_limit_bytes=16 * MIB),
        cost_estimate=pl.CostEstimate(flops=2 * rows * D * D, bytes_accessed=4 * D * D, transcendentals=0),
        name="project_queries",
    )(gain, w_query, *parts)


def attend_kernel(chunk, owned, flag, queries, *refs):
    keys, values, out = refs[:SPLIT], refs[SPLIT : 2 * SPLIT], refs[-1]
    rows = queries.shape[0]
    count = values[0].shape[0]
    step = pl.program_id(0)
    pairs = HEADS // 2
    part = PART
    low = lax.broadcasted_iota(jnp.int32, (1, 128), 1) < HEAD_DIM

    def place(pair):
        begin = pair * 128 % (D // SPLIT)
        return pair * 128 // (D // SPLIT), slice(begin, begin + 128)

    def attention(causal, count):
        lane = lax.broadcasted_iota(jnp.int32, (rows, 128), 1)
        lse = jnp.zeros((rows, 128), jnp.float32)
        ones = jnp.ones((count, 128), jnp.bfloat16)
        if causal:
            key_pos = lax.broadcasted_iota(jnp.int32, (rows, count), 1)
            row = step * rows + lax.broadcasted_iota(jnp.int32, (rows, count), 0)
            query_pos = (row // part) * owned + chunk * part + row % part
            allowed = key_pos <= query_pos
            allowed = jnp.concatenate([allowed, allowed], axis=0)

        def scores_of(pair):
            at = slice(pair * 128, (pair + 1) * 128)
            query = queries[:, at]
            none = jnp.zeros_like(query)
            both = jnp.concatenate([jnp.where(low, query, none), jnp.where(low, none, query)], axis=0)
            block, features = place(pair)
            scores = jnp.dot(both, keys[block][features, 0:count], preferred_element_type=jnp.float32)
            return jnp.where(allowed, scores, MASKED) if causal else scores

        ahead = scores_of(0)
        for pair in range(pairs):
            at = slice(pair * 128, (pair + 1) * 128)
            scores = ahead
            if pair + 1 < pairs:
                ahead = scores_of(pair + 1)
            block, features = place(pair)
            top = jnp.max(scores, axis=-1, keepdims=True)
            weights = jnp.exp2((scores - top) * EXP2_SCALE).astype(jnp.bfloat16)
            mixed = jnp.dot(
                weights,
                jnp.concatenate([values[block][0:count, features], ones], axis=1),
                preferred_element_type=jnp.float32,
            )
            mix, total = mixed[:, 0:128], mixed[:, 128:256]
            both = jnp.where(low, mix[:rows], mix[rows:]) / jnp.where(low, total[:rows], total[rows:])
            out[:, at] = both.astype(jnp.bfloat16)
            level = top * EXP2_SCALE + jnp.log2(total)
            lse = jnp.where(lane == 2 * pair, level[:rows], lse)
            lse = jnp.where(lane == 2 * pair + 1, level[rows:], lse)
        first = lse.astype(jnp.bfloat16).astype(jnp.float32)
        second = (lse - first).astype(jnp.bfloat16).astype(jnp.float32)
        third = lse - first - second
        pieces = first + pltpu.roll(second, HEADS, 1) + pltpu.roll(third, 2 * HEADS, 1)
        out[:, D:WIDE] = pieces.astype(jnp.bfloat16)

    @pl.when(flag[0] == 0)
    def _():
        attention(False, count)

    @pl.when(jnp.logical_and(flag[0] != 0, step == 0))
    def _():
        attention(True, rows // part * owned)

    @pl.when(jnp.logical_and(flag[0] != 0, step != 0))
    def _():
        attention(True, count)


def attend(chunk, owned, is_last, queries, keys, values):
    count = queries.shape[0]
    rows = 256
    key_block = lambda i, c: (i, 0)
    value_block = lambda i, c: (0, i)
    block = lambda c: (c, 0)
    return pl.pallas_call(
        functools.partial(attend_kernel, chunk, owned),
        grid=(count // rows,),
        out_shape=jax.ShapeDtypeStruct((count, WIDE), jnp.bfloat16),
        in_specs=[
            pl.BlockSpec(memory_space=pltpu.SMEM),
            pl.BlockSpec((rows, D), block),
        ]
        + [pl.BlockSpec((D // SPLIT, keys.shape[1]), functools.partial(key_block, i)) for i in range(SPLIT)]
        + [pl.BlockSpec((values.shape[0], D // SPLIT), functools.partial(value_block, i)) for i in range(SPLIT)],
        out_specs=pl.BlockSpec((rows, WIDE), block),
        compiler_params=pltpu.CompilerParams(vmem_limit_bytes=56 * MIB),
        cost_estimate=pl.CostEstimate(
            flops=16 * count * D * D, bytes_accessed=8 * D * D, transcendentals=HEADS * count * D
        ),
        name="attend_%d" % chunk,
    )(is_last, queries, *([keys] * SPLIT), *([values] * SPLIT))


def finish_kernel(number, *refs):
    parts, (own, gain, w_out, out) = refs[:number], refs[number:]
    head = lax.broadcasted_iota(jnp.int32, (128, D), 0)
    column = lax.broadcasted_iota(jnp.int32, (128, D), 1)
    spread = (column // HEAD_DIM == head).astype(jnp.bfloat16)
    spread = jnp.concatenate([spread, spread], axis=0)
    posts = []
    for each in parts:
        count, part, _ = each.shape
        lane = lax.broadcasted_iota(jnp.int32, (count * part, 128), 1)
        pieces = each[:, :, D:WIDE].astype(jnp.float32).reshape(count * part, 128)
        level = pieces + pltpu.roll(pieces, 128 - HEADS, 1) + pltpu.roll(pieces, 128 - 2 * HEADS, 1)
        level = jnp.where(lane < HEADS, level, 0.0).reshape(count, part, 128)
        weight = jnp.exp2(level - jnp.max(level, axis=0, keepdims=True))
        weight = weight / jnp.sum(weight, axis=0, keepdims=True)
        weight = weight.reshape(count * part, 128)
        high = weight.astype(jnp.bfloat16)
        rest = (weight - high.astype(jnp.float32)).astype(jnp.bfloat16)
        wide = jnp.dot(
            jnp.concatenate([high, rest], axis=1), spread, preferred_element_type=jnp.float32
        ).reshape(count, part, D)
        mix = jnp.sum(wide * each[:, :, 0:D].astype(jnp.float32), axis=0)
        posts.append(rms_rows(mix.astype(jnp.bfloat16), gain[...]))
    mixed = own[...].astype(jnp.float32) + jnp.dot(
        jnp.concatenate(posts, axis=0), w_out[...], preferred_element_type=jnp.float32
    )
    out[...] = mixed.astype(jnp.bfloat16)


def finish(parts, own, gain, w_out):
    rows = own.shape[0]
    return pl.pallas_call(
        functools.partial(finish_kernel, len(parts)),
        out_shape=jax.ShapeDtypeStruct((rows, D), jnp.bfloat16),
        compiler_params=pltpu.CompilerParams(vmem_limit_bytes=28 * MIB),
        cost_estimate=pl.CostEstimate(flops=4 * rows * D * D, bytes_accessed=8 * D * D, transcendentals=0),
        name="finish",
    )(*parts, own, gain, w_out)


def pack_kernel(owned, source, flag, tokens, own, *bundles):
    def block(to):
        return tokens[to * owned : (to + 1) * owned, :]

    mine = block(source)
    own[...] = jnp.where(flag[0] != 0, mine, jnp.zeros_like(mine))
    for members, bundle in zip(BUNDLES, bundles):
        for place in range(4):
            at = slice(place * owned, (place + 1) * owned)
            bundle[at, :] = block(members[min(place, len(members) - 1)])


def relay_kernel(*refs):
    bundles, outs = refs[:4], refs[4:]
    rows = outs[0].shape[0]
    for place, out in enumerate(outs):
        at = slice(place * rows, (place + 1) * rows)
        total = bundles[0][at, :].astype(jnp.float32)
        for bundle in bundles[1:]:
            total = total + bundle[at, :].astype(jnp.float32)
        out[...] = total.astype(jnp.bfloat16)


def scatter(tokens, owned, source, flag, beside):
    limit = pltpu.CompilerParams(vmem_limit_bytes=16 * MIB)
    block = jax.ShapeDtypeStruct((owned, D), jnp.bfloat16)
    smem = pl.BlockSpec(memory_space=pltpu.SMEM)
    vmem = pl.BlockSpec(memory_space=pltpu.VMEM)
    own, *bundles = pl.pallas_call(
        functools.partial(pack_kernel, owned, source),
        out_shape=(block,) + (jax.ShapeDtypeStruct((4 * owned, D), jnp.bfloat16),) * 4,
        in_specs=[smem, vmem],
        compiler_params=limit,
        cost_estimate=pl.CostEstimate(flops=0, bytes_accessed=8 * D * D, transcendentals=0),
        name="pack",
    )(flag, tokens)
    bundles = [
        lax.ppermute(bundle, "seq", [(source, members[0])]) for members, bundle in zip(BUNDLES, bundles)
    ]
    bundles, _ = lax.optimization_barrier((bundles, beside))
    kept, *passed = pl.pallas_call(
        relay_kernel,
        out_shape=(block,) * 4,
        compiler_params=limit,
        cost_estimate=pl.CostEstimate(flops=0, bytes_accessed=4 * D * D, transcendentals=0),
        name="relay",
    )(*bundles)
    parts = [own, kept]
    for place in range(1, 4):
        pairs = [(members[0], members[place]) for members in BUNDLES if place < len(members)]
        parts.append(lax.ppermute(passed[place - 1], "seq", pairs))
    return parts


def local(tokens, ln_gain, post_gain, w_query, w_key, w_value, w_out):
    count = lax.axis_size("seq")
    last = lax.axis_index("seq") == count - 1
    flag = last.astype(jnp.int32).reshape(1)
    owned = LATENTS // count
    gain = ln_gain.reshape(1, D)
    keys, values = project_kv(tokens, gain, w_key, w_value)
    parts = scatter(tokens, owned, count - 1, flag, keys)
    own, tiled_a, tiled_b = project_queries(count, gain, w_query, parts)
    rows_a = lax.all_to_all(tiled_a, "seq", 0, 0)
    rows_a, tiled_b = lax.optimization_barrier((rows_a, tiled_b))
    rows_b = lax.all_to_all(tiled_b, "seq", 0, 0)
    mixed_a = attend(0, owned, flag, rows_a.reshape(-1, D), keys, values)
    rows_b, _ = lax.optimization_barrier((rows_b, mixed_a))
    mixed_b = attend(1, owned, flag, rows_b.reshape(-1, D), keys, values)
    mixed = [lax.all_to_all(each.reshape(count, PART, WIDE), "seq", 0, 0) for each in (mixed_a, mixed_b)]
    return finish(mixed, own, post_gain.reshape(1, D), w_out)


def solution(mesh):
    return jax.shard_map(
        local,
        mesh=mesh,
        in_specs=(P(("ctx", "seq"), None), P(), P(), P(), P(), P(), P()),
        out_specs=P(("ctx", "seq"), None),
        check_vma=False,
    )
```

```python
import functools

import jax
import jax.numpy as jnp
from jax import lax
from jax.experimental import pallas as pl
from jax.experimental.pallas import tpu as pltpu
from jax.sharding import PartitionSpec as P

D = 1024
HEADS = 16
HEAD_DIM = 64
PAIRS = HEADS // 2
LATENTS = 1024
PART = 32
SPLIT = 4
LOG2E = 1.4426950408889634
EXP2_SCALE = LOG2E * HEAD_DIM ** (-0.5)
MASKED = -1e30
WIDE = D + 128
MIB = 2**20

BUNDLES = ((3, 0, 2, 1), (11, 8, 10, 9), (12, 13, 4, 5), (14, 6, 7))


def rms_rows(rows, gain):
    wide = rows.astype(jnp.float32)
    scale = lax.rsqrt(jnp.mean(wide * wide, axis=-1, keepdims=True) + 1e-06)
    return (wide * scale * gain).astype(jnp.bfloat16)


def kv_kernel(tokens, gain, w_key, w_value, keys, values, normed):
    @pl.when(pl.program_id(0) == 0)
    def _():
        normed[...] = rms_rows(tokens[...], gain[...])

    rows = normed[...]
    keys[...] = jnp.dot(rows, w_key[...], preferred_element_type=jnp.float32).astype(jnp.bfloat16)
    values[...] = jnp.dot(rows, w_value[...], preferred_element_type=jnp.float32).T.astype(jnp.bfloat16)


def project_kv(tokens, gain, w_key, w_value):
    rows = tokens.shape[0]
    cols = 256
    whole = lambda c: (0, 0)
    block = lambda c: (0, c)
    return pl.pallas_call(
        kv_kernel,
        grid=(D // cols,),
        out_shape=(
            jax.ShapeDtypeStruct((rows, D), jnp.bfloat16),
            jax.ShapeDtypeStruct((D, rows), jnp.bfloat16),
        ),
        in_specs=[
            pl.BlockSpec((rows, D), whole, pipeline_mode=pl.Buffered(1)),
            pl.BlockSpec((1, D), whole),
            pl.BlockSpec((D, cols), block),
            pl.BlockSpec((D, cols), block),
        ],
        out_specs=(pl.BlockSpec((rows, cols), block), pl.BlockSpec((cols, rows), lambda c: (c, 0))),
        scratch_shapes=[pltpu.VMEM((rows, D), jnp.bfloat16)],
        compiler_params=pltpu.CompilerParams(vmem_limit_bytes=56 * MIB),
        cost_estimate=pl.CostEstimate(flops=4 * rows * D * D, bytes_accessed=10 * rows * D, transcendentals=0),
        name="project_kv",
    )(tokens, gain, w_key, w_value)


def query_kernel(count, gain, w_query, *refs):
    parts, (own, *tiled) = refs[:5], refs[5:]
    rows = parts[0][...].astype(jnp.float32)
    for part in parts[1:]:
        rows = rows + part[...].astype(jnp.float32)
    rows = rows.astype(jnp.bfloat16)
    own[...] = rows
    queries = jnp.dot(
        rms_rows(rows, gain[...]), w_query[...], preferred_element_type=jnp.float32
    ).astype(jnp.bfloat16)
    begin = 0
    for each in tiled:
        end = begin + each.shape[1]
        for to in range(count):
            each[to] = queries[begin:end]
        begin = end


def project_queries(count, gain, w_query, parts):
    rows = parts[0].shape[0]
    return pl.pallas_call(
        functools.partial(query_kernel, count),
        out_shape=(jax.ShapeDtypeStruct((rows, D), jnp.bfloat16),)
        + tuple(jax.ShapeDtypeStruct((count, each, D), jnp.bfloat16) for each in (PART, rows - PART)),
        compiler_params=pltpu.CompilerParams(vmem_limit_bytes=16 * MIB),
        cost_estimate=pl.CostEstimate(flops=2 * rows * D * D, bytes_accessed=4 * D * D, transcendentals=0),
        name="project_queries",
    )(gain, w_query, *parts)


def attend_kernel(chunk, owned, flag, queries, *refs):
    keys, values, out = refs[:SPLIT], refs[SPLIT : 2 * SPLIT], refs[-1]
    rows = queries.shape[0]
    count = keys[0].shape[0]
    step = pl.program_id(0)
    pairs = HEADS // 2
    part = PART
    low = lax.broadcasted_iota(jnp.int32, (1, 128), 1) < HEAD_DIM

    def attention(causal, count):
        ones = jnp.ones((16, count), jnp.bfloat16)
        if causal:
            key_pos = lax.broadcasted_iota(jnp.int32, (count, rows), 0)
            row = step * rows + lax.broadcasted_iota(jnp.int32, (count, rows), 1)
            query_pos = (row // part) * owned + chunk * part + row % part
            allowed = key_pos <= query_pos
            allowed = jnp.concatenate([allowed, allowed], axis=1)

        def scores_of(pair):
            query = queries[:, pair * 128 : (pair + 1) * 128]
            none = jnp.zeros_like(query)
            both = jnp.concatenate([jnp.where(low, query, none), jnp.where(low, none, query)], axis=0)
            begin = pair * 128 % (D // SPLIT)
            key = keys[pair * 128 // (D // SPLIT)][0:count, begin : begin + 128]
            scores = lax.dot_general(key, both, (((1,), (1,)), ((), ())), preferred_element_type=jnp.float32)
            return jnp.where(allowed, scores, MASKED) if causal else scores

        levels = []
        ahead = scores_of(0)
        for pair in range(pairs):
            scores = ahead
            if pair + 1 < pairs:
                ahead = scores_of(pair + 1)
            top = jnp.max(scores, axis=0, keepdims=True)
            weights = jnp.exp2((scores - top) * EXP2_SCALE).astype(jnp.bfloat16)
            halves = []
            for half in range(2):
                begin = (pair * 128 + half * HEAD_DIM) % (D // SPLIT)
                value = values[pair * 128 // (D // SPLIT)][begin : begin + HEAD_DIM, 0:count]
                across = slice(half * rows, (half + 1) * rows)
                mixed = jnp.dot(
                    jnp.concatenate([value, ones], axis=0),
                    weights[:, across],
                    preferred_element_type=jnp.float32,
                )
                total = mixed[HEAD_DIM : HEAD_DIM + 1]
                halves.append(mixed[:HEAD_DIM] / total)
                levels.append(top[:, across] * EXP2_SCALE + jnp.log2(total))
            mix = jnp.concatenate(halves, axis=0).T
            out[:, pair * 128 : (pair + 1) * 128] = mix.astype(jnp.bfloat16)
        levels.append(jnp.zeros((128 - HEADS, rows), jnp.float32))
        lse = jnp.concatenate(levels, axis=0).T
        first = lse.astype(jnp.bfloat16).astype(jnp.float32)
        second = (lse - first).astype(jnp.bfloat16).astype(jnp.float32)
        third = lse - first - second
        pieces = first + pltpu.roll(second, HEADS, 1) + pltpu.roll(third, 2 * HEADS, 1)
        out[:, D:WIDE] = pieces.astype(jnp.bfloat16)

    @pl.when(flag[0] == 0)
    def _():
        attention(False, count)

    @pl.when(jnp.logical_and(flag[0] != 0, step == 0))
    def _():
        attention(True, rows // part * owned)

    @pl.when(jnp.logical_and(flag[0] != 0, step != 0))
    def _():
        attention(True, count)


def attend(chunk, owned, is_last, queries, keys, values):
    count = queries.shape[0]
    rows = 256
    key_block = lambda i, c: (0, i)
    value_block = lambda i, c: (i, 0)
    block = lambda c: (c, 0)
    return pl.pallas_call(
        functools.partial(attend_kernel, chunk, owned),
        grid=(count // rows,),
        out_shape=jax.ShapeDtypeStruct((count, WIDE), jnp.bfloat16),
        in_specs=[
            pl.BlockSpec(memory_space=pltpu.SMEM),
            pl.BlockSpec((rows, D), block),
        ]
        + [pl.BlockSpec((keys.shape[0], D // SPLIT), functools.partial(key_block, i)) for i in range(SPLIT)]
        + [pl.BlockSpec((D // SPLIT, values.shape[1]), functools.partial(value_block, i)) for i in range(SPLIT)],
        out_specs=pl.BlockSpec((rows, WIDE), block),
        compiler_params=pltpu.CompilerParams(vmem_limit_bytes=56 * MIB),
        cost_estimate=pl.CostEstimate(
            flops=16 * count * D * D, bytes_accessed=8 * D * D, transcendentals=HEADS * count * D
        ),
        name="attend_%d" % chunk,
    )(is_last, queries, *([keys] * SPLIT), *([values] * SPLIT))


def finish_kernel(number, *refs):
    parts, (own, gain, w_out, out) = refs[:number], refs[number:]
    head = lax.broadcasted_iota(jnp.int32, (128, D), 0)
    column = lax.broadcasted_iota(jnp.int32, (128, D), 1)
    spread = (column // HEAD_DIM == head).astype(jnp.bfloat16)
    spread = jnp.concatenate([spread, spread], axis=0)
    posts = []
    for each in parts:
        count, part, _ = each.shape
        lane = lax.broadcasted_iota(jnp.int32, (count * part, 128), 1)
        pieces = each[:, :, D:WIDE].astype(jnp.float32).reshape(count * part, 128)
        level = pieces + pltpu.roll(pieces, 128 - HEADS, 1) + pltpu.roll(pieces, 128 - 2 * HEADS, 1)
        level = jnp.where(lane < HEADS, level, 0.0).reshape(count, part, 128)
        weight = jnp.exp2(level - jnp.max(level, axis=0, keepdims=True))
        weight = weight / jnp.sum(weight, axis=0, keepdims=True)
        weight = weight.reshape(count * part, 128)
        high = weight.astype(jnp.bfloat16)
        rest = (weight - high.astype(jnp.float32)).astype(jnp.bfloat16)
        wide = jnp.dot(
            jnp.concatenate([high, rest], axis=1), spread, preferred_element_type=jnp.float32
        ).reshape(count, part, D)
        mix = jnp.sum(wide * each[:, :, 0:D].astype(jnp.float32), axis=0)
        posts.append(rms_rows(mix.astype(jnp.bfloat16), gain[...]))
    mixed = own[...].astype(jnp.float32) + jnp.dot(
        jnp.concatenate(posts, axis=0), w_out[...], preferred_element_type=jnp.float32
    )
    out[...] = mixed.astype(jnp.bfloat16)


def finish(parts, own, gain, w_out):
    rows = own.shape[0]
    return pl.pallas_call(
        functools.partial(finish_kernel, len(parts)),
        out_shape=jax.ShapeDtypeStruct((rows, D), jnp.bfloat16),
        compiler_params=pltpu.CompilerParams(vmem_limit_bytes=28 * MIB),
        cost_estimate=pl.CostEstimate(flops=4 * rows * D * D, bytes_accessed=8 * D * D, transcendentals=0),
        name="finish",
    )(*parts, own, gain, w_out)


def pack_kernel(owned, source, flag, tokens, own, *bundles):
    def block(to):
        return tokens[to * owned : (to + 1) * owned, :]

    mine = block(source)
    own[...] = jnp.where(flag[0] != 0, mine, jnp.zeros_like(mine))
    for members, bundle in zip(BUNDLES, bundles):
        for place in range(4):
            at = slice(place * owned, (place + 1) * owned)
            bundle[at, :] = block(members[min(place, len(members) - 1)])


def relay_kernel(*refs):
    bundles, outs = refs[:4], refs[4:]
    rows = outs[0].shape[0]
    for place, out in enumerate(outs):
        at = slice(place * rows, (place + 1) * rows)
        total = bundles[0][at, :].astype(jnp.float32)
        for bundle in bundles[1:]:
            total = total + bundle[at, :].astype(jnp.float32)
        out[...] = total.astype(jnp.bfloat16)


def scatter(tokens, owned, source, flag, beside):
    limit = pltpu.CompilerParams(vmem_limit_bytes=16 * MIB)
    block = jax.ShapeDtypeStruct((owned, D), jnp.bfloat16)
    smem = pl.BlockSpec(memory_space=pltpu.SMEM)
    vmem = pl.BlockSpec(memory_space=pltpu.VMEM)
    own, *bundles = pl.pallas_call(
        functools.partial(pack_kernel, owned, source),
        out_shape=(block,) + (jax.ShapeDtypeStruct((4 * owned, D), jnp.bfloat16),) * 4,
        in_specs=[smem, vmem],
        compiler_params=limit,
        cost_estimate=pl.CostEstimate(flops=0, bytes_accessed=8 * D * D, transcendentals=0),
        name="pack",
    )(flag, tokens)
    bundles = [
        lax.ppermute(bundle, "seq", [(source, members[0])]) for members, bundle in zip(BUNDLES, bundles)
    ]
    bundles, _ = lax.optimization_barrier((bundles, beside))
    kept, *passed = pl.pallas_call(
        relay_kernel,
        out_shape=(block,) * 4,
        compiler_params=limit,
        cost_estimate=pl.CostEstimate(flops=0, bytes_accessed=4 * D * D, transcendentals=0),
        name="relay",
    )(*bundles)
    parts = [own, kept]
    for place in range(1, 4):
        pairs = [(members[0], members[place]) for members in BUNDLES if place < len(members)]
        parts.append(lax.ppermute(passed[place - 1], "seq", pairs))
    return parts


def local(tokens, ln_gain, post_gain, w_query, w_key, w_value, w_out):
    count = lax.axis_size("seq")
    last = lax.axis_index("seq") == count - 1
    flag = last.astype(jnp.int32).reshape(1)
    owned = LATENTS // count
    gain = ln_gain.reshape(1, D)
    keys, values = project_kv(tokens, gain, w_key, w_value)
    parts = scatter(tokens, owned, count - 1, flag, keys)
    own, tiled_a, tiled_b = project_queries(count, gain, w_query, parts)
    rows_a = lax.all_to_all(tiled_a, "seq", 0, 0)
    rows_a, tiled_b = lax.optimization_barrier((rows_a, tiled_b))
    rows_b = lax.all_to_all(tiled_b, "seq", 0, 0)
    mixed_a = attend(0, owned, flag, rows_a.reshape(-1, D), keys, values)
    rows_b, _ = lax.optimization_barrier((rows_b, mixed_a))
    mixed_b = attend(1, owned, flag, rows_b.reshape(-1, D), keys, values)
    mixed = [lax.all_to_all(each.reshape(count, PART, WIDE), "seq", 0, 0) for each in (mixed_a, mixed_b)]
    return finish(mixed, own, post_gain.reshape(1, D), w_out)


def solution(mesh):
    return jax.shard_map(
        local,
        mesh=mesh,
        in_specs=(P(("ctx", "seq"), None), P(), P(), P(), P(), P(), P()),
        out_specs=P(("ctx", "seq"), None),
        check_vma=False,
    )
```

```python
import functools

import jax
import jax.numpy as jnp
from jax import lax
from jax.experimental import pallas as pl
from jax.experimental.pallas import tpu as pltpu
from jax.sharding import PartitionSpec as P

D = 1024
HEADS = 16
HEAD_DIM = 64
PAIRS = HEADS // 2
LATENTS = 1024
PART = 32
SPLIT = 4
LOG2E = 1.4426950408889634
EXP2_SCALE = LOG2E * HEAD_DIM ** (-0.5)
MASKED = -1e30
WIDE = D + 128
MIB = 2**20

BUNDLES = ((12, 0, 8, 13), (14, 2, 10), (3, 1, 5, 7), (11, 9, 4, 6))


def rms_rows(rows, gain):
    wide = rows.astype(jnp.float32)
    scale = lax.rsqrt(jnp.mean(wide * wide, axis=-1, keepdims=True) + 1e-06)
    return (wide * scale * gain).astype(jnp.bfloat16)


def kv_kernel(tokens, gain, w_key, w_value, keys, values, normed):
    @pl.when(pl.program_id(0) == 0)
    def _():
        normed[...] = rms_rows(tokens[...], gain[...])

    rows = normed[...]
    keys[...] = jnp.dot(rows, w_key[...], preferred_element_type=jnp.float32).T.astype(jnp.bfloat16)
    values[...] = jnp.dot(rows, w_value[...], preferred_element_type=jnp.float32).astype(jnp.bfloat16)


def project_kv(tokens, gain, w_key, w_value):
    rows = tokens.shape[0]
    cols = 256
    whole = lambda c: (0, 0)
    block = lambda c: (0, c)
    return pl.pallas_call(
        kv_kernel,
        grid=(D // cols,),
        out_shape=(
            jax.ShapeDtypeStruct((D, rows), jnp.bfloat16),
            jax.ShapeDtypeStruct((rows, D), jnp.bfloat16),
        ),
        in_specs=[
            pl.BlockSpec((rows, D), whole, pipeline_mode=pl.Buffered(1)),
            pl.BlockSpec((1, D), whole),
            pl.BlockSpec((D, cols), block),
            pl.BlockSpec((D, cols), block),
        ],
        out_specs=(pl.BlockSpec((cols, rows), lambda c: (c, 0)), pl.BlockSpec((rows, cols), block)),
        scratch_shapes=[pltpu.VMEM((rows, D), jnp.bfloat16)],
        compiler_params=pltpu.CompilerParams(vmem_limit_bytes=56 * MIB),
        cost_estimate=pl.CostEstimate(flops=4 * rows * D * D, bytes_accessed=10 * rows * D, transcendentals=0),
        name="project_kv",
    )(tokens, gain, w_key, w_value)


def query_kernel(count, gain, w_query, *refs):
    parts, (own, *tiled) = refs[:5], refs[5:]
    rows = parts[0][...].astype(jnp.float32)
    for part in parts[1:]:
        rows = rows + part[...].astype(jnp.float32)
    rows = rows.astype(jnp.bfloat16)
    own[...] = rows
    queries = jnp.dot(
        rms_rows(rows, gain[...]), w_query[...], preferred_element_type=jnp.float32
    ).astype(jnp.bfloat16)
    begin = 0
    for each in tiled:
        end = begin + each.shape[1]
        for to in range(count):
            each[to] = queries[begin:end]
        begin = end


def project_queries(count, gain, w_query, parts):
    rows = parts[0].shape[0]
    return pl.pallas_call(
        functools.partial(query_kernel, count),
        out_shape=(jax.ShapeDtypeStruct((rows, D), jnp.bfloat16),)
        + tuple(jax.ShapeDtypeStruct((count, each, D), jnp.bfloat16) for each in (PART, rows - PART)),
        compiler_params=pltpu.CompilerParams(vmem_limit_bytes=16 * MIB),
        cost_estimate=pl.CostEstimate(flops=2 * rows * D * D, bytes_accessed=4 * D * D, transcendentals=0),
        name="project_queries",
    )(gain, w_query, *parts)


def attend_kernel(chunk, owned, flag, queries, *refs):
    keys, values, out = refs[:SPLIT], refs[SPLIT : 2 * SPLIT], refs[-1]
    pairs = HEADS // 2
    part = PART
    low = lax.broadcasted_iota(jnp.int32, (1, 128), 1) < HEAD_DIM

    def place(pair):
        begin = pair * 128 % (D // SPLIT)
        return pair * 128 // (D // SPLIT), slice(begin, begin + 128)

    def attention(causal, start, rows, count):
        mine = slice(start, start + rows)
        lane = lax.broadcasted_iota(jnp.int32, (rows, 128), 1)
        lse = jnp.zeros((rows, 128), jnp.float32)
        ones = jnp.ones((count, 128), jnp.bfloat16)
        if causal:
            key_pos = lax.broadcasted_iota(jnp.int32, (rows, count), 1)
            row = start + lax.broadcasted_iota(jnp.int32, (rows, count), 0)
            query_pos = (row // part) * owned + chunk * part + row % part
            allowed = key_pos <= query_pos
            allowed = jnp.concatenate([allowed, allowed], axis=0)

        def scores_of(pair):
            at = slice(pair * 128, (pair + 1) * 128)
            query = queries[mine, at]
            none = jnp.zeros_like(query)
            both = jnp.concatenate([jnp.where(low, query, none), jnp.where(low, none, query)], axis=0)
            block, features = place(pair)
            scores = jnp.dot(both, keys[block][features, 0:count], preferred_element_type=jnp.float32)
            return jnp.where(allowed, scores, MASKED) if causal else scores

        ahead = scores_of(0)
        for pair in range(pairs):
            at = slice(pair * 128, (pair + 1) * 128)
            scores = ahead
            if pair + 1 < pairs:
                ahead = scores_of(pair + 1)
            block, features = place(pair)
            top = jnp.max(scores, axis=-1, keepdims=True)
            weights = jnp.exp2((scores - top) * EXP2_SCALE).astype(jnp.bfloat16)
            mixed = jnp.dot(
                weights,
                jnp.concatenate([values[block][0:count, features], ones], axis=1),
                preferred_element_type=jnp.float32,
            )
            mix, total = mixed[:, 0:128], mixed[:, 128:256]
            both = jnp.where(low, mix[:rows], mix[rows:]) / jnp.where(low, total[:rows], total[rows:])
            out[mine, at] = both.astype(jnp.bfloat16)
            level = top * EXP2_SCALE + jnp.log2(total)
            lse = jnp.where(lane == 2 * pair, level[:rows], lse)
            lse = jnp.where(lane == 2 * pair + 1, level[rows:], lse)
        first = lse.astype(jnp.bfloat16).astype(jnp.float32)
        second = (lse - first).astype(jnp.bfloat16).astype(jnp.float32)
        third = lse - first - second
        pieces = first + pltpu.roll(second, HEADS, 1) + pltpu.roll(third, 2 * HEADS, 1)
        out[mine, D:WIDE] = pieces.astype(jnp.bfloat16)

    rows = queries.shape[0]
    count = values[0].shape[0]

    @pl.when(flag[0] == 0)
    def _():
        attention(False, 0, rows, count)

    @pl.when(flag[0] != 0)
    def _():
        attention(True, 0, rows // 2, rows // 2 // part * owned)
        attention(True, rows // 2, rows // 2, count)


def attend(chunk, owned, is_last, queries, keys, values):
    count = queries.shape[0]
    rows = count
    key_block = lambda i, c: (i, 0)
    value_block = lambda i, c: (0, i)
    block = lambda c: (c, 0)
    return pl.pallas_call(
        functools.partial(attend_kernel, chunk, owned),
        grid=(count // rows,),
        out_shape=jax.ShapeDtypeStruct((count, WIDE), jnp.bfloat16),
        in_specs=[
            pl.BlockSpec(memory_space=pltpu.SMEM),
            pl.BlockSpec((rows, D), block),
        ]
        + [pl.BlockSpec((D // SPLIT, keys.shape[1]), functools.partial(key_block, i)) for i in range(SPLIT)]
        + [pl.BlockSpec((values.shape[0], D // SPLIT), functools.partial(value_block, i)) for i in range(SPLIT)],
        out_specs=pl.BlockSpec((rows, WIDE), block),
        compiler_params=pltpu.CompilerParams(vmem_limit_bytes=56 * MIB),
        cost_estimate=pl.CostEstimate(
            flops=16 * count * D * D, bytes_accessed=8 * D * D, transcendentals=HEADS * count * D
        ),
        name="attend_%d" % chunk,
    )(is_last, queries, *([keys] * SPLIT), *([values] * SPLIT))


def finish_kernel(number, *refs):
    parts, (own, gain, w_out, out) = refs[:number], refs[number:]
    head = lax.broadcasted_iota(jnp.int32, (128, D), 0)
    column = lax.broadcasted_iota(jnp.int32, (128, D), 1)
    spread = (column // HEAD_DIM == head).astype(jnp.bfloat16)
    spread = jnp.concatenate([spread, spread], axis=0)
    posts = []
    for each in parts:
        count, part, _ = each.shape
        lane = lax.broadcasted_iota(jnp.int32, (count * part, 128), 1)
        pieces = each[:, :, D:WIDE].astype(jnp.float32).reshape(count * part, 128)
        level = pieces + pltpu.roll(pieces, 128 - HEADS, 1) + pltpu.roll(pieces, 128 - 2 * HEADS, 1)
        level = jnp.where(lane < HEADS, level, 0.0).reshape(count, part, 128)
        weight = jnp.exp2(level - jnp.max(level, axis=0, keepdims=True))
        weight = weight / jnp.sum(weight, axis=0, keepdims=True)
        weight = weight.reshape(count * part, 128)
        high = weight.astype(jnp.bfloat16)
        rest = (weight - high.astype(jnp.float32)).astype(jnp.bfloat16)
        wide = jnp.dot(
            jnp.concatenate([high, rest], axis=1), spread, preferred_element_type=jnp.float32
        ).reshape(count, part, D)
        mix = jnp.sum(wide * each[:, :, 0:D].astype(jnp.float32), axis=0)
        posts.append(rms_rows(mix.astype(jnp.bfloat16), gain[...]))
    mixed = own[...].astype(jnp.float32) + jnp.dot(
        jnp.concatenate(posts, axis=0), w_out[...], preferred_element_type=jnp.float32
    )
    out[...] = mixed.astype(jnp.bfloat16)


def finish(parts, own, gain, w_out):
    rows = own.shape[0]
    return pl.pallas_call(
        functools.partial(finish_kernel, len(parts)),
        out_shape=jax.ShapeDtypeStruct((rows, D), jnp.bfloat16),
        compiler_params=pltpu.CompilerParams(vmem_limit_bytes=28 * MIB),
        cost_estimate=pl.CostEstimate(flops=4 * rows * D * D, bytes_accessed=8 * D * D, transcendentals=0),
        name="finish",
    )(*parts, own, gain, w_out)


def pack_kernel(owned, source, flag, tokens, own, *bundles):
    def block(to):
        return tokens[to * owned : (to + 1) * owned, :]

    mine = block(source)
    own[...] = jnp.where(flag[0] != 0, mine, jnp.zeros_like(mine))
    for members, bundle in zip(BUNDLES, bundles):
        for place, member in enumerate(members):
            bundle[place * owned : (place + 1) * owned, :] = block(member)


def relay_kernel(*refs):
    bundles, outs = refs[:4], refs[4:]
    rows = outs[0].shape[0]
    for place, out in enumerate(outs):
        at = slice(place * rows, (place + 1) * rows)
        held = [bundle[at, :].astype(jnp.float32) for bundle in bundles if place * rows < bundle.shape[0]]
        out[...] = sum(held[1:], held[0]).astype(jnp.bfloat16)


def scatter(tokens, owned, source, flag, beside):
    limit = pltpu.CompilerParams(vmem_limit_bytes=16 * MIB)
    block = jax.ShapeDtypeStruct((owned, D), jnp.bfloat16)
    smem = pl.BlockSpec(memory_space=pltpu.SMEM)
    vmem = pl.BlockSpec(memory_space=pltpu.VMEM)
    own, *bundles = pl.pallas_call(
        functools.partial(pack_kernel, owned, source),
        out_shape=(block,) + tuple(jax.ShapeDtypeStruct((len(members) * owned, D), jnp.bfloat16) for members in BUNDLES),
        in_specs=[smem, vmem],
        compiler_params=limit,
        cost_estimate=pl.CostEstimate(flops=0, bytes_accessed=8 * D * D, transcendentals=0),
        name="pack",
    )(flag, tokens)
    bundles = [
        lax.ppermute(bundle, "seq", [(source, members[0])]) for members, bundle in zip(BUNDLES, bundles)
    ]
    bundles, _ = lax.optimization_barrier((bundles, beside))
    kept, *passed = pl.pallas_call(
        relay_kernel,
        out_shape=(block,) * 4,
        compiler_params=limit,
        cost_estimate=pl.CostEstimate(flops=0, bytes_accessed=4 * D * D, transcendentals=0),
        name="relay",
    )(*bundles)
    parts = [own, kept]
    for place in range(1, 4):
        pairs = [(members[0], members[place]) for members in BUNDLES if place < len(members)]
        parts.append(lax.ppermute(passed[place - 1], "seq", pairs))
    return parts


def local(tokens, ln_gain, post_gain, w_query, w_key, w_value, w_out):
    count = lax.axis_size("seq")
    last = lax.axis_index("seq") == count - 1
    flag = last.astype(jnp.int32).reshape(1)
    owned = LATENTS // count
    gain = ln_gain.reshape(1, D)
    keys, values = project_kv(tokens, gain, w_key, w_value)
    parts = scatter(tokens, owned, count - 1, flag, keys)
    own, tiled_a, tiled_b = project_queries(count, gain, w_query, parts)
    rows_a = lax.all_to_all(tiled_a, "seq", 0, 0)
    rows_a, tiled_b = lax.optimization_barrier((rows_a, tiled_b))
    rows_b = lax.all_to_all(tiled_b, "seq", 0, 0)
    mixed_a = attend(0, owned, flag, rows_a.reshape(-1, D), keys, values)
    rows_b, _ = lax.optimization_barrier((rows_b, mixed_a))
    mixed_b = attend(1, owned, flag, rows_b.reshape(-1, D), keys, values)
    mixed = [lax.all_to_all(each.reshape(count, PART, WIDE), "seq", 0, 0) for each in (mixed_a, mixed_b)]
    return finish(mixed, own, post_gain.reshape(1, D), w_out)


def solution(mesh):
    return jax.shard_map(
        local,
        mesh=mesh,
        in_specs=(P(("ctx", "seq"), None), P(), P(), P(), P(), P(), P()),
        out_specs=P(("ctx", "seq"), None),
        check_vma=False,
    )
```

```python
import functools

import jax
import jax.numpy as jnp
from jax import lax
from jax.experimental import pallas as pl
from jax.experimental.pallas import tpu as pltpu
from jax.sharding import PartitionSpec as P

D = 1024
HEADS = 16
HEAD_DIM = 64
PAIRS = HEADS // 2
LATENTS = 1024
PART = 32
SPLIT = 4
LOG2E = 1.4426950408889634
EXP2_SCALE = LOG2E * HEAD_DIM ** (-0.5)
MASKED = -1e30
WIDE = D + 128
MIB = 2**20

BUNDLES = ((12, 0, 8, 13), (14, 2, 10), (3, 1, 5, 7), (11, 9, 4, 6))


def rms_rows(rows, gain):
    wide = rows.astype(jnp.float32)
    scale = lax.rsqrt(jnp.mean(wide * wide, axis=-1, keepdims=True) + 1e-06)
    return (wide * scale * gain).astype(jnp.bfloat16)


def kv_kernel(tokens, gain, w_key, w_value, keys, values, normed):
    @pl.when(pl.program_id(0) == 0)
    def _():
        normed[...] = rms_rows(tokens[...], gain[...])

    rows = normed[...]
    keys[...] = jnp.dot(rows, w_key[...], preferred_element_type=jnp.float32).T.astype(jnp.bfloat16)
    values[...] = jnp.dot(rows, w_value[...], preferred_element_type=jnp.float32).astype(jnp.bfloat16)


def project_kv(tokens, gain, w_key, w_value):
    rows = tokens.shape[0]
    cols = 256
    whole = lambda c: (0, 0)
    block = lambda c: (0, c)
    return pl.pallas_call(
        kv_kernel,
        grid=(D // cols,),
        out_shape=(
            jax.ShapeDtypeStruct((D, rows), jnp.bfloat16),
            jax.ShapeDtypeStruct((rows, D), jnp.bfloat16),
        ),
        in_specs=[
            pl.BlockSpec((rows, D), whole, pipeline_mode=pl.Buffered(1)),
            pl.BlockSpec((1, D), whole),
            pl.BlockSpec((D, cols), block),
            pl.BlockSpec((D, cols), block),
        ],
        out_specs=(pl.BlockSpec((cols, rows), lambda c: (c, 0)), pl.BlockSpec((rows, cols), block)),
        scratch_shapes=[pltpu.VMEM((rows, D), jnp.bfloat16)],
        compiler_params=pltpu.CompilerParams(vmem_limit_bytes=56 * MIB),
        cost_estimate=pl.CostEstimate(flops=4 * rows * D * D, bytes_accessed=10 * rows * D, transcendentals=0),
        name="project_kv",
    )(tokens, gain, w_key, w_value)


def query_kernel(count, gain, w_query, *refs):
    parts, (own, *tiled) = refs[:5], refs[5:]
    rows = parts[0][...].astype(jnp.float32)
    for part in parts[1:]:
        rows = rows + part[...].astype(jnp.float32)
    rows = rows.astype(jnp.bfloat16)
    own[...] = rows
    queries = jnp.dot(
        rms_rows(rows, gain[...]), w_query[...], preferred_element_type=jnp.float32
    ).astype(jnp.bfloat16)
    begin = 0
    for each in tiled:
        end = begin + each.shape[1]
        for to in range(count):
            each[to] = queries[begin:end]
        begin = end


def project_queries(count, gain, w_query, parts):
    rows = parts[0].shape[0]
    return pl.pallas_call(
        functools.partial(query_kernel, count),
        out_shape=(jax.ShapeDtypeStruct((rows, D), jnp.bfloat16),)
        + tuple(jax.ShapeDtypeStruct((count, each, D), jnp.bfloat16) for each in (PART, rows - PART)),
        compiler_params=pltpu.CompilerParams(vmem_limit_bytes=16 * MIB),
        cost_estimate=pl.CostEstimate(flops=2 * rows * D * D, bytes_accessed=4 * D * D, transcendentals=0),
        name="project_queries",
    )(gain, w_query, *parts)


def attend_kernel(chunk, owned, flag, queries, *refs):
    keys, values, out = refs[:SPLIT], refs[SPLIT : 2 * SPLIT], refs[-1]
    rows = queries.shape[0]
    count = values[0].shape[0]
    step = pl.program_id(0)
    pairs = HEADS // 2
    part = PART
    low = lax.broadcasted_iota(jnp.int32, (1, 128), 1) < HEAD_DIM

    def place(pair):
        begin = pair * 128 % (D // SPLIT)
        return pair * 128 // (D // SPLIT), slice(begin, begin + 128)

    def attention(causal, count):
        lane = lax.broadcasted_iota(jnp.int32, (rows, 128), 1)
        lse = jnp.zeros((rows, 128), jnp.float32)
        ones = jnp.ones((count, 128), jnp.bfloat16)
        if causal:
            key_pos = lax.broadcasted_iota(jnp.int32, (rows, count), 1)
            row = step * rows + lax.broadcasted_iota(jnp.int32, (rows, count), 0)
            query_pos = (row // part) * owned + chunk * part + row % part
            allowed = key_pos <= query_pos
            allowed = jnp.concatenate([allowed, allowed], axis=0)

        def scores_of(pair):
            at = slice(pair * 128, (pair + 1) * 128)
            query = queries[:, at]
            none = jnp.zeros_like(query)
            both = jnp.concatenate([jnp.where(low, query, none), jnp.where(low, none, query)], axis=0)
            block, features = place(pair)
            scores = jnp.dot(both, keys[block][features, 0:count], preferred_element_type=jnp.float32)
            return jnp.where(allowed, scores, MASKED) if causal else scores

        ahead = scores_of(0)
        for pair in range(pairs):
            at = slice(pair * 128, (pair + 1) * 128)
            scores = ahead
            if pair + 1 < pairs:
                ahead = scores_of(pair + 1)
            block, features = place(pair)
            top = jnp.max(scores, axis=-1, keepdims=True)
            weights = jnp.exp2((scores - top) * EXP2_SCALE).astype(jnp.bfloat16)
            mixed = jnp.dot(
                weights,
                jnp.concatenate([values[block][0:count, features], ones], axis=1),
                preferred_element_type=jnp.float32,
            )
            mix, total = mixed[:, 0:128], mixed[:, 128:256]
            both = jnp.where(low, mix[:rows], mix[rows:]) / jnp.where(low, total[:rows], total[rows:])
            out[:, at] = both.astype(jnp.bfloat16)
            level = top * EXP2_SCALE + jnp.log2(total)
            lse = jnp.where(lane == 2 * pair, level[:rows], lse)
            lse = jnp.where(lane == 2 * pair + 1, level[rows:], lse)
        first = lse.astype(jnp.bfloat16).astype(jnp.float32)
        second = (lse - first).astype(jnp.bfloat16).astype(jnp.float32)
        third = lse - first - second
        pieces = first + pltpu.roll(second, HEADS, 1) + pltpu.roll(third, 2 * HEADS, 1)
        out[:, D:WIDE] = pieces.astype(jnp.bfloat16)

    @pl.when(flag[0] == 0)
    def _():
        attention(False, count)

    @pl.when(jnp.logical_and(flag[0] != 0, step == 0))
    def _():
        attention(True, rows // part * owned)

    @pl.when(jnp.logical_and(flag[0] != 0, step != 0))
    def _():
        attention(True, count)


def attend(chunk, owned, is_last, queries, keys, values):
    count = queries.shape[0]
    rows = 256
    key_block = lambda i, c: (i, 0)
    value_block = lambda i, c: (0, i)
    block = lambda c: (c, 0)
    return pl.pallas_call(
        functools.partial(attend_kernel, chunk, owned),
        grid=(count // rows,),
        out_shape=jax.ShapeDtypeStruct((count, WIDE), jnp.bfloat16),
        in_specs=[
            pl.BlockSpec(memory_space=pltpu.SMEM),
            pl.BlockSpec((rows, D), block),
        ]
        + [pl.BlockSpec((D // SPLIT, keys.shape[1]), functools.partial(key_block, i)) for i in range(SPLIT)]
        + [pl.BlockSpec((values.shape[0], D // SPLIT), functools.partial(value_block, i)) for i in range(SPLIT)],
        out_specs=pl.BlockSpec((rows, WIDE), block),
        compiler_params=pltpu.CompilerParams(vmem_limit_bytes=56 * MIB),
        cost_estimate=pl.CostEstimate(
            flops=16 * count * D * D, bytes_accessed=8 * D * D, transcendentals=HEADS * count * D
        ),
        name="attend_%d" % chunk,
    )(is_last, queries, *([keys] * SPLIT), *([values] * SPLIT))


def finish_kernel(number, *refs):
    parts, (own, gain, w_out, out) = refs[:number], refs[number:]
    head = lax.broadcasted_iota(jnp.int32, (128, D), 0)
    column = lax.broadcasted_iota(jnp.int32, (128, D), 1)
    spread = (column // HEAD_DIM == head).astype(jnp.bfloat16)
    spread = jnp.concatenate([spread, spread], axis=0)
    posts = []
    for each in parts:
        count, part, _ = each.shape
        lane = lax.broadcasted_iota(jnp.int32, (count * part, 128), 1)
        pieces = each[:, :, D:WIDE].astype(jnp.float32).reshape(count * part, 128)
        level = pieces + pltpu.roll(pieces, 128 - HEADS, 1) + pltpu.roll(pieces, 128 - 2 * HEADS, 1)
        level = jnp.where(lane < HEADS, level, 0.0).reshape(count, part, 128)
        weight = jnp.exp2(level - jnp.max(level, axis=0, keepdims=True))
        weight = weight / jnp.sum(weight, axis=0, keepdims=True)
        weight = weight.reshape(count * part, 128)
        high = weight.astype(jnp.bfloat16)
        rest = (weight - high.astype(jnp.float32)).astype(jnp.bfloat16)
        wide = jnp.dot(
            jnp.concatenate([high, rest], axis=1), spread, preferred_element_type=jnp.float32
        ).reshape(count, part, D)
        mix = jnp.sum(wide * each[:, :, 0:D].astype(jnp.float32), axis=0)
        posts.append(rms_rows(mix.astype(jnp.bfloat16), gain[...]))
    mixed = own[...].astype(jnp.float32) + jnp.dot(
        jnp.concatenate(posts, axis=0), w_out[...], preferred_element_type=jnp.float32
    )
    out[...] = mixed.astype(jnp.bfloat16)


def finish(parts, own, gain, w_out):
    rows = own.shape[0]
    return pl.pallas_call(
        functools.partial(finish_kernel, len(parts)),
        out_shape=jax.ShapeDtypeStruct((rows, D), jnp.bfloat16),
        compiler_params=pltpu.CompilerParams(vmem_limit_bytes=28 * MIB),
        cost_estimate=pl.CostEstimate(flops=4 * rows * D * D, bytes_accessed=8 * D * D, transcendentals=0),
        name="finish",
    )(*parts, own, gain, w_out)


def pack_kernel(owned, source, flag, tokens, own, *bundles):
    def block(to):
        return tokens[to * owned : (to + 1) * owned, :]

    mine = block(source)
    own[...] = jnp.where(flag[0] != 0, mine, jnp.zeros_like(mine))
    for members, bundle in zip(BUNDLES, bundles):
        for place, member in enumerate(members):
            bundle[place * owned : (place + 1) * owned, :] = block(member)


def relay_kernel(*refs):
    bundles, outs = refs[:4], refs[4:]
    rows = outs[0].shape[0]
    for place, out in enumerate(outs):
        at = slice(place * rows, (place + 1) * rows)
        held = [bundle[at, :].astype(jnp.float32) for bundle in bundles if place * rows < bundle.shape[0]]
        out[...] = sum(held[1:], held[0]).astype(jnp.bfloat16)


def scatter(tokens, owned, source, flag, beside):
    limit = pltpu.CompilerParams(vmem_limit_bytes=16 * MIB)
    block = jax.ShapeDtypeStruct((owned, D), jnp.bfloat16)
    smem = pl.BlockSpec(memory_space=pltpu.SMEM)
    vmem = pl.BlockSpec(memory_space=pltpu.VMEM)
    own, *bundles = pl.pallas_call(
        functools.partial(pack_kernel, owned, source),
        out_shape=(block,) + tuple(jax.ShapeDtypeStruct((len(members) * owned, D), jnp.bfloat16) for members in BUNDLES),
        in_specs=[smem, vmem],
        compiler_params=limit,
        cost_estimate=pl.CostEstimate(flops=0, bytes_accessed=8 * D * D, transcendentals=0),
        name="pack",
    )(flag, tokens)
    bundles = [
        lax.ppermute(bundle, "seq", [(source, members[0])]) for members, bundle in zip(BUNDLES, bundles)
    ]
    bundles, _ = lax.optimization_barrier((bundles, beside))
    kept, *passed = pl.pallas_call(
        relay_kernel,
        out_shape=(block,) * 4,
        compiler_params=limit,
        cost_estimate=pl.CostEstimate(flops=0, bytes_accessed=4 * D * D, transcendentals=0),
        name="relay",
    )(*bundles)
    parts = [own, kept]
    for place in range(1, 4):
        pairs = [(members[0], members[place]) for members in BUNDLES if place < len(members)]
        parts.append(lax.ppermute(passed[place - 1], "seq", pairs))
    return parts


def local(tokens, ln_gain, post_gain, w_query, w_key, w_value, w_out):
    count = lax.axis_size("seq")
    last = lax.axis_index("seq") == count - 1
    flag = last.astype(jnp.int32).reshape(1)
    owned = LATENTS // count
    gain = ln_gain.reshape(1, D)
    keys, values = project_kv(tokens, gain, w_key, w_value)
    parts = scatter(tokens, owned, count - 1, flag, keys)
    own, tiled_a, tiled_b = project_queries(count, gain, w_query, parts)
    rows_a = lax.all_to_all(tiled_a, "seq", 0, 0)
    rows_a, tiled_b = lax.optimization_barrier((rows_a, tiled_b))
    rows_b = lax.all_to_all(tiled_b, "seq", 0, 0)
    mixed_a = attend(0, owned, flag, rows_a.reshape(-1, D), keys, values)
    rows_b, _ = lax.optimization_barrier((rows_b, mixed_a))
    mixed_b = attend(1, owned, flag, rows_b.reshape(-1, D), keys, values)
    mixed = [lax.all_to_all(each.reshape(count, PART, WIDE), "seq", 0, 0) for each in (mixed_a, mixed_b)]
    return finish(mixed, own, post_gain.reshape(1, D), w_out)


def solution(mesh):
    return jax.shard_map(
        local,
        mesh=mesh,
        in_specs=(P(("ctx", "seq"), None), P(), P(), P(), P(), P(), P()),
        out_specs=P(("ctx", "seq"), None),
        check_vma=False,
    )
```
